128 devices in a mesh: depth: 2 (over core), rows: 2 (over x_hi), shots: 32 (over z, y, x_lo).
Axes of the slice: x: 4 (x_hi: 2, x_lo: 2; x = x_hi * 2 + x_lo), y: 4, z: 4, core: 2. Of those that a mesh axis runs over, the one named last changes fastest.
Arguments:
- sources: float32 [2, 2, 1024, 4096], P('depth', None, 'rows', 'shots'), may hold values from -6 to 6
- factor: float32 [2, 2, 1024, 1024], P('depth', None, ('rows', 'shots')), may hold values from -0.09375 to 0.09375
- block_mask: int32 [2, 2, 8, 8], P('depth'), may hold values 0 or 1
- inverse_diagonal: float32 [2, 2, 1024, 1024], P('depth', None, None, 'rows'), may hold values from -1.2 to 1.2, as said below
Outputs:
- solution: float32 [2, 2, 1024, 4096], P('depth', None, 'rows', 'shots')
The draws below stay inside these ranges and needn't reach their ends.
Inputs may be any that keep to these rules, and one draw needn't show every extreme that they name: Each block inverse_diagonal[d, m] is lower triangular with diagonal entries between 0.8 and 1.2.
All inputs are finite; a program needn't handle non-finite values. No bound on the sum of `block_mask` on one device may be relied on, other than what follows from the above.
Results may differ from the reference program's by a relative error of at most 0.0001.
Values sent between devices are 32-bit elements; how exact they have to be, the bound alone decides.
A program may use at most 64 MiB of HBM per device.

```python
import jax
import jax.numpy as jnp
from jax import lax

SUPER = 1024
BLOCK = 128
NRHS = 4096
LEVELS = 2
PAIRS = 2
N_DEPTH = 2


def draw_inverse_diagonal(key, part):
    shape = (N_DEPTH, LEVELS, SUPER, SUPER)
    first_key = jax.random.fold_in(key, 11)
    second_key = jax.random.fold_in(key, 23)
    noise = jax.random.normal(first_key, shape, jnp.float32)
    diagonal_values = jax.random.uniform(second_key, (N_DEPTH, LEVELS, SUPER, 1), jnp.float32, 0.8, 1.2)
    identity = jnp.eye(SUPER, dtype=jnp.float32)
    strict = jnp.tril(noise, -1) * (0.7 / SUPER ** 0.5)
    return strict + identity * diagonal_values


def place_ends(values, rng, smallest, high):
    longest = values.shape.index(max(values.shape))
    spots = []
    for shift in (0, 1):
        where = [jax.random.randint(jax.random.fold_in(rng, axis), (), 0, length) for axis, length in enumerate(values.shape)]
        where[longest] = (where[longest] + shift) % values.shape[longest]
        spots.append(tuple(where))
    return values.at[spots[0]].set(smallest).at[spots[1]].set(high)


def block_scale(stream_key, dims, pieces, low, largest):
    level, own = 1.0, jax.random.fold_in(stream_key, 6)
    for dim, blocks in pieces:
        steps = jnp.exp(jax.random.uniform(jax.random.fold_in(own, dim), (blocks,), jnp.float32, low / len(pieces), largest / len(pieces)))
        level = level * jnp.repeat(steps, dims[dim] // blocks).reshape([-1 if axis == dim else 1 for axis in range(len(dims))])
    return level


def normal_values(own_key, dims, deviation, most, pieces=(), kind=jnp.bfloat16):
    result = deviation * jax.random.normal(own_key, dims, jnp.float32)
    if pieces:
        result = result * block_scale(own_key, dims, pieces, -0.22, 0.18)
    return jnp.clip(result, -most, most).astype(kind)


def setup_inputs(seed: int = 0) -> dict:
    key_list = jax.random.split(jax.random.key(seed), 5)
    return {
        "sources": normal_values(key_list[0], (N_DEPTH, LEVELS, SUPER, NRHS), 1.0, 6.0, ((0, 2), (2, 2), (3, 32)), jnp.float32),
        "factor": normal_values(key_list[1], (N_DEPTH, PAIRS, SUPER, SUPER), (2 * SUPER * N_DEPTH) ** -0.5, 0.09375, ((0, 2), (2, 64)), jnp.float32),
        "block_mask": place_ends((jax.random.randint(key_list[2], (N_DEPTH, PAIRS, SUPER // BLOCK, SUPER // BLOCK), 0, 4) < 3).astype(jnp.int32), jax.random.fold_in(key_list[2], 1), 0, 1),
        "inverse_diagonal": draw_inverse_diagonal(jax.random.fold_in(key_list[4], 71), 0),
    }


def pair_offset(lower_level, upper_level):
    offset = 0
    for earlier in range(1, upper_level):
        offset = offset + earlier * 2 ** earlier
    return offset + lower_level * 2 ** upper_level


def masked_tile(factor, block_mask, device, offset):
    expand = jnp.repeat(jnp.repeat(block_mask[device, offset].astype(jnp.float32), BLOCK, axis=0), BLOCK, axis=1)
    return factor[device, offset] * expand


def product(left, right):
    return jnp.dot(left, right, precision=lax.Precision.HIGHEST, preferred_element_type=jnp.float32)


def reference(sources, factor, block_mask, inverse_diagonal):
    forward_solved = {}
    for upper_level in range(LEVELS):
        group_size = 2 ** upper_level
        for device in range(N_DEPTH):
            group_start = (device // group_size) * group_size
            position = device - group_start
            remaining = sources[device, upper_level]
            for lower_level in range(upper_level):
                offset = pair_offset(lower_level, upper_level) + position
                for member in range(group_start, group_start + group_size):
                    factor_tile = masked_tile(factor, block_mask, member, offset)
                    remaining = remaining - product(factor_tile, forward_solved[(lower_level, member)])
            forward_solved[(upper_level, device)] = product(inverse_diagonal[device, upper_level], remaining)
    backward_solved = {}
    for lower_level in reversed(range(LEVELS)):
        for device in range(N_DEPTH):
            remaining = forward_solved[(lower_level, device)]
            for upper_level in range(lower_level + 1, LEVELS):
                group_size = 2 ** upper_level
                group_start = (device // group_size) * group_size
                for position in range(group_size):
                    offset = pair_offset(lower_level, upper_level) + position
                    factor_tile = masked_tile(factor, block_mask, device, offset)
                    remaining = remaining - product(factor_tile.T, backward_solved[(upper_level, group_start + position)])
            backward_solved[(lower_level, device)] = product(inverse_diagonal[device, lower_level].T, remaining)
    return jnp.stack([jnp.stack([backward_solved[(tier_index, device)] for tier_index in range(LEVELS)]) for device in range(N_DEPTH)])
```

```python
import jax
import jax.numpy as jnp
from jax import lax
from jax.sharding import PartitionSpec as P


def mask_rows(factor_rows, block_mask, row_start, block_size):
    row_total = factor_rows.shape[1]
    block_count = block_mask.shape[3]
    row_blocks = (row_start + jnp.arange(row_total, dtype=jnp.int32)) // block_size
    row_select = (row_blocks[:, None] == jnp.arange(block_count, dtype=jnp.int32)[None, :]).astype(
        jnp.float32
    )
    row_masks = jnp.einsum("rk,pkc->prc", row_select, block_mask[0].astype(jnp.float32))
    return factor_rows * jnp.repeat(row_masks, block_size, axis=2)


def product(spec, left, right):
    return jnp.einsum(
        spec, left, right, precision=lax.Precision.HIGH, preferred_element_type=jnp.float32
    )


def per_device(sources, factor, block_mask, inverse_diagonal):
    shot_index = lax.axis_index("shots")
    rows_index = lax.axis_index("rows")
    thin_rows = factor.shape[2]
    full_width = factor.shape[3]
    block_size = full_width // block_mask.shape[3]
    row_start = (rows_index * lax.axis_size("shots") + shot_index) * thin_rows
    masked = mask_rows(factor[0], block_mask, row_start, block_size)
    tiles = lax.all_gather(masked, "shots", axis=1, tiled=True)
    low = lax.psum(product("rs,sn->rn", inverse_diagonal[0, 0], sources[0, 0]), "rows")
    update = product("trs,sn->trn", tiles, low)
    own = sources[0, 1] - lax.psum_scatter(update, "depth", scatter_dimension=0, tiled=True)[0]
    high = lax.psum(product("rs,sn->rn", inverse_diagonal[0, 1], own), "rows")
    top = product("sr,sn->rn", inverse_diagonal[0, 1], high)
    tops = lax.all_gather(top[None], "depth", axis=0, tiled=True)
    target = low - lax.psum(product("trs,trn->sn", tiles, tops), "rows")
    bottom = product("sr,sn->rn", inverse_diagonal[0, 0], target)
    return jnp.stack([bottom, top])[None]


def solution(mesh):
    placed = (
        P("depth", None, "rows", "shots"),
        P("depth", None, ("rows", "shots"), None),
        P("depth", None, None, None),
        P("depth", None, None, "rows"),
    )
    return jax.shard_map(
        per_device,
        mesh=mesh,
        in_specs=placed,
        out_specs=P("depth", None, "rows", "shots"),
        check_vma=False,
    )
```

```python
import jax
import jax.numpy as jnp
from jax import lax
from jax.experimental import pallas as pl
from jax.experimental.pallas import tpu as pltpu
from jax.sharding import PartitionSpec as P

MESH = pl.DeviceIdType.MESH
F32 = jnp.float32
BF16 = jnp.bfloat16
BLOCK = 128
HALF = 512
FULL = 1024
SHOTS = 128


def split(x):
    high = x.astype(BF16)
    return high, (x - high.astype(F32)).astype(BF16)


def dot(a, b):
    return jnp.dot(a, b, preferred_element_type=F32)


def wide_product(a_high, a_low, b_pair):
    both = dot(a_high, b_pair)
    return both[:, :SHOTS] + both[:, SHOTS:] + dot(a_low, b_pair[:, :SHOTS])


def tall_product(a_pair, b_high, b_low):
    both = dot(a_pair, b_high)
    return both[:SHOTS] + both[SHOTS:] + dot(a_pair[:SHOTS], b_low)


class Copies:
    def __init__(self, send_sems, recv_sems):
        self.send_sems, self.recv_sems, self.count, self.sent = send_sems, recv_sems, 0, []

    def slot(self):
        self.count += 1
        return self.count - 1

    def make(self, slot, src, dst, device):
        return pltpu.make_async_remote_copy(
            src_ref=src,
            dst_ref=dst,
            send_sem=self.send_sems.at[slot],
            recv_sem=self.recv_sems.at[slot],
            device_id=device,
            device_id_type=MESH,
        )

    def send(self, slot, src, dst, device):
        copy = self.make(slot, src, dst, device)
        copy.start()
        self.sent.append(copy)

    def arrived(self, slot, dst, device):
        self.make(slot, dst, dst, device).wait_recv()

    def finish(self):
        for copy in self.sent:
            copy.wait_send()


COPIES = 104


def kernel(
    src_hbm,
    fac_hbm,
    mask_ref,
    inv_hbm,
    out_ref,
    src,
    fac,
    inv,
    tiles,
    tiles_high,
    tiles_low,
    inv_high,
    inv_low,
    low,
    low_in,
    low_pair,
    low_t,
    update,
    update_in,
    high_out,
    high_in,
    top_t,
    part_t,
    part_in,
    load_sems,
    send_sems,
    recv_sems,
):
    core = lax.axis_index("depth")
    row = lax.axis_index("rows")
    shot = lax.axis_index("shots")
    zy, xl = shot // 2, shot % 2
    z, y = zy // 4, zy % 4

    def at(dz, dy):
        return ((z + dz) % 4) * 4 + (y + dy) % 4

    def place(axis, step):
        return at(step, 0) if axis == 0 else at(0, step)

    def neighbour(axis, step):
        return (core, row, place(axis, step) * 2 + xl)

    beside = (core, row, zy * 2 + 1 - xl)
    across = (core, 1 - row, shot)
    twin = (1 - core, row, shot)

    loads = [
        pltpu.make_async_copy(fac_hbm.at[0], fac, load_sems.at[0]),
        pltpu.make_async_copy(src_hbm.at[0], src, load_sems.at[1]),
        pltpu.make_async_copy(inv_hbm.at[0, 0], inv.at[0], load_sems.at[2]),
        pltpu.make_async_copy(inv_hbm.at[0, 1], inv.at[1], load_sems.at[3]),
    ]
    for load in loads:
        load.start()

    barrier = pltpu.get_barrier_semaphore()
    partners = [neighbour(a, s) for a in (0, 1) for s in (1, -1)] + [beside, across, twin]
    for partner in partners:
        pl.semaphore_signal(barrier, inc=1, device_id=partner, device_id_type=MESH)

    loads[0].wait()
    row_block = row * 4 + zy // 4
    for t in range(2):
        for k in range(8):
            scale = mask_ref[0, t, row_block, k].astype(F32)
            piece = fac[t, :, k * BLOCK : (k + 1) * BLOCK] * scale
            tiles[t, k // 4, zy, xl, :, (k % 4) * BLOCK : (k % 4 + 1) * BLOCK] = piece

    pl.semaphore_wait(barrier, len(partners))

    copies = Copies(send_sems, recv_sems)
    parts = [(t, h) for t in range(2) for h in range(2)]
    first = {h: 1 - h for h in range(2)}
    slot_x = {p: copies.slot() for p in parts}
    slot_own = {(p, s): copies.slot() for p in parts for s in (1, -1)}
    slot_side = {(p, s): copies.slot() for p in parts for s in (1, -1)}
    slot_far = {(p, s): copies.slot() for p in parts for s in (1, -1)}
    units = (0, -1, 1, 2)
    slot_two = {(p, u, s): copies.slot() for p in parts for u in units for s in (1, -1)}
    slot_two_far = {(p, u, s): copies.slot() for p in parts for u in units for s in (1, -1)}
    slot_low = [copies.slot() for _ in range(2)]
    slot_update = copies.slot()
    slot_high = copies.slot()
    slot_top = copies.slot()
    slot_part = [copies.slot() for _ in range(4)]
    assert copies.count <= COPIES

    def unit_place(h, u, s):
        return at(s, u) if first[h] == 1 else at(u, s)

    def swap_beside(p):
        t, h = p
        piece = tiles.at[t, h, zy, xl]
        copies.send(slot_x[p], piece, piece, beside)

    def send_own(p):
        t, h = p
        piece = tiles.at[t, h, zy, xl]
        for s in (1, -1):
            copies.send(slot_own[p, s], piece, piece, neighbour(first[h], s))

    def wait_beside(p):
        t, h = p
        copies.arrived(slot_x[p], tiles.at[t, h, zy, 1 - xl], beside)

    def send_side(p):
        t, h = p
        piece = tiles.at[t, h, zy, 1 - xl]
        for s in (1, -1):
            copies.send(slot_side[p, s], piece, piece, neighbour(first[h], s))

    def send_unit(p, u):
        t, h = p
        piece = tiles.at[t, h, unit_place(h, u, 0)]
        for s in (1, -1):
            copies.send(slot_two[p, u, s], piece, piece, neighbour(1 - first[h], s))

    def relay_one(p, s):
        t, h = p
        where = unit_place(h, -s, 0)
        copies.arrived(slot_own[p, s], tiles.at[t, h, where, xl], neighbour(first[h], -s))
        copies.arrived(slot_side[p, s], tiles.at[t, h, where, 1 - xl], neighbour(first[h], -s))
        piece = tiles.at[t, h, where, 0 if s == 1 else 1]
        copies.send(slot_far[p, s], piece, piece, neighbour(first[h], s))

    def wait_far(p):
        t, h = p
        for s in (1, -1):
            piece = tiles.at[t, h, unit_place(h, 2, 0), 0 if s == 1 else 1]
            copies.arrived(slot_far[p, s], piece, neighbour(first[h], -s))

    def relay_two(p, u):
        t, h = p
        for s in (1, -1):
            where = unit_place(h, u, -s)
            copies.arrived(slot_two[p, u, s], tiles.at[t, h, where], neighbour(1 - first[h], -s))
            piece = tiles.at[t, h, where, 0 if s == 1 else 1]
            copies.send(slot_two_far[p, u, s], piece, piece, neighbour(1 - first[h], s))

    def wait_two_far(p, u):
        t, h = p
        for s in (1, -1):
            piece = tiles.at[t, h, unit_place(h, u, 2), 0 if s == 1 else 1]
            copies.arrived(slot_two_far[p, u, s], piece, neighbour(1 - first[h], -s))

    def pair(t):
        return [(t, 0), (t, 1)]

    for p in parts:
        swap_beside(p)
    for p in pair(0):
        send_own(p)

    def invert_split(m):
        loads[2 + m].wait()

        @pl.loop(0, 4)
        def _(i):
            rows = pl.ds(pl.multiple_of(i * 256, 256), 256)
            inv_high[m, rows], inv_low[m, rows] = split(inv[m, rows])

    loads[1].wait()
    invert_split(0)
    for p in pair(0):
        wait_beside(p)
        send_side(p)
        send_unit(p, 0)
    source_pair = jnp.concatenate(split(src[0]), axis=1)

    @pl.loop(0, 4)
    def _(i):
        rows = pl.ds(pl.multiple_of(i * 256, 256), 256)
        low[rows] = wide_product(inv_high[0, rows], inv_low[0, rows], source_pair)

    bottom, upper = pl.ds(HALF, HALF), pl.ds(0, HALF)
    copies.send(slot_low[1], low.at[bottom], low_in.at[bottom], across)

    @pl.when(row == 0)
    def _():
        copies.make(slot_low[0], low.at[upper], low_in.at[upper], across).start()

    for p in pair(0):
        for s in (1, -1):
            relay_one(p, s)
        send_unit(p, -1)
        send_unit(p, 1)
    for p in pair(1):
        send_own(p)
        wait_beside(p)
        send_side(p)
        send_unit(p, 0)
    for p in pair(0):
        wait_far(p)
        send_unit(p, 2)
    invert_split(1)
    for p in pair(0):
        relay_two(p, 0)
    for p in pair(1):
        for s in (1, -1):
            relay_one(p, s)
        send_unit(p, -1)
        send_unit(p, 1)
    for p in pair(0):
        relay_two(p, -1)
        relay_two(p, 1)
    for p in pair(1):
        wait_far(p)
        send_unit(p, 2)
    for p in pair(0):
        relay_two(p, 2)
    for p in pair(1):
        relay_two(p, 0)

    copies.arrived(slot_low[1], low_in.at[bottom], across)

    @pl.when(row == 1)
    def _():
        copies.arrived(slot_low[0], low_in.at[upper], across)

    @pl.when(row == 0)
    def _():
        low_in[upper] = low[upper]

    low_in[bottom] = low[bottom] + low_in[bottom]
    low_pair[...] = jnp.concatenate(split(low_in[...]), axis=1)
    low_t[...] = low_in[...].T

    for p in pair(1):
        relay_two(p, -1)
        relay_two(p, 1)

    def forward(t):
        @pl.loop(0, 4)
        def _(i):
            rows = pl.ds(pl.multiple_of(i * 128, 128), 128)
            total = jnp.zeros((128, SHOTS), F32)
            for h in range(2):
                block = tiles[t, h, pl.ds(i * 4, 4)].reshape(128, HALF)
                high, rest = split(block)
                cols = pl.ds(h * HALF, HALF)
                tiles_high[t, rows, cols] = high
                tiles_low[t, rows, cols] = rest
                total += wide_product(high, rest, low_pair[cols])
            update[t, rows] = total

    def level_one(t):
        @pl.when(core != t)
        def _():
            copy = copies.make(slot_update, update.at[t], update_in, twin)
            copy.start()
            copy.wait_send()
            copies.arrived(slot_top, top_t, twin)

        @pl.when(core == t)
        def _():
            copies.arrived(slot_update, update_in, twin)
            own_pair = jnp.concatenate(split(src[1] - update[t] - update_in[...]), axis=1)

            @pl.loop(0, 4)
            def _(i):
                rows = pl.ds(pl.multiple_of(i * 256, 256), 256)
                high_out[rows] = wide_product(inv_high[1, rows], inv_low[1, rows], own_pair)

            copy = copies.make(slot_high, high_out.at[bottom], high_in, across)
            copy.start()
            upper_pair = jnp.concatenate(split(high_out[upper].T), axis=0)
            total = tall_product(upper_pair, inv_high[1, upper], inv_low[1, upper])
            copy.wait()
            lower_pair = jnp.concatenate(split((high_out[bottom] + high_in[...]).T), axis=0)
            total += tall_product(lower_pair, inv_high[1, bottom], inv_low[1, bottom])
            top_t[...] = total
            copy = copies.make(slot_top, top_t, top_t, twin)
            copy.start()
            out_ref[0, 1] = total.T
            copy.wait_send()

    def backward(t):
        top_pair = jnp.concatenate(split(top_t[...]), axis=0)
        for k in range(4):
            cols = pl.ds(k * 256, 256)
            share = tall_product(top_pair, tiles_high[t, :, cols], tiles_low[t, :, cols])
            part_t[k] = share if t == 0 else part_t[k] + share

    for p in pair(0):
        for u in units:
            wait_two_far(p, u)
    for p in pair(1):
        relay_two(p, 2)
    for p in pair(1):
        for u in units:
            wait_two_far(p, u)
    for t in range(2):
        forward(t)
    for t in range(2):
        level_one(t)
        backward(t)

    for k in (2, 3):
        copies.send(slot_part[k], part_t.at[k], part_in.at[k], across)

    @pl.when(row == 1)
    def _():
        for k in (0, 1):
            copies.make(slot_part[k], part_t.at[k], part_in.at[k], across).start()

    def final(k):
        cols = pl.ds(k * 256, 256)
        copies.arrived(slot_part[k], part_in.at[k], across)
        target = low_t[:, cols] - part_t[k] - part_in[k]
        pair_ = jnp.concatenate(split(target), axis=0)
        return tall_product(pair_, inv_high[0, cols], inv_low[0, cols])

    answer = final(2) + final(3)
    low_in[pl.ds(0, HALF)] = answer.T

    @pl.when(row == 0)
    def _():
        more = final(0) + final(1)
        low_in[pl.ds(0, HALF)] = low_in[pl.ds(0, HALF)] + more.T

    out_ref[0, 0] = low_in[pl.ds(0, HALF)]

    copies.finish()

    @pl.when(row == 0)
    def _():
        copies.make(slot_low[0], low.at[upper], low_in.at[upper], across).wait_send()

    @pl.when(row == 1)
    def _():
        for k in (0, 1):
            copies.make(slot_part[k], part_t.at[k], part_in.at[k], across).wait_send()


def per_device(sources, factor, block_mask, inverse_diagonal):
    return pl.pallas_call(
        kernel,
        out_shape=jax.ShapeDtypeStruct(sources.shape, F32),
        in_specs=[
            pl.BlockSpec(memory_space=pl.ANY),
            pl.BlockSpec(memory_space=pl.ANY),
            pl.BlockSpec(memory_space=pltpu.SMEM),
            pl.BlockSpec(memory_space=pl.ANY),
        ],
        out_specs=pl.BlockSpec(memory_space=pltpu.VMEM),
        scratch_shapes=[
            pltpu.VMEM((2, HALF, SHOTS), F32),
            pltpu.VMEM((2, 16, FULL), F32),
            pltpu.VMEM((2, FULL, HALF), F32),
            pltpu.VMEM((2, 2, 16, 2, 16, HALF), F32),
            pltpu.VMEM((2, HALF, FULL), BF16),
            pltpu.VMEM((2, HALF, FULL), BF16),
            pltpu.VMEM((2, FULL, HALF), BF16),
            pltpu.VMEM((2, FULL, HALF), BF16),
            pltpu.VMEM((FULL, SHOTS), F32),
            pltpu.VMEM((FULL, SHOTS), F32),
            pltpu.VMEM((FULL, 2 * SHOTS), BF16),
            pltpu.VMEM((SHOTS, FULL), F32),
            pltpu.VMEM((2, HALF, SHOTS), F32),
            pltpu.VMEM((HALF, SHOTS), F32),
            pltpu.VMEM((FULL, SHOTS), F32),
            pltpu.VMEM((HALF, SHOTS), F32),
            pltpu.VMEM((SHOTS, HALF), F32),
            pltpu.VMEM((4, SHOTS, 256), F32),
            pltpu.VMEM((4, SHOTS, 256), F32),
            pltpu.SemaphoreType.DMA((4,)),
            pltpu.SemaphoreType.DMA((COPIES,)),
            pltpu.SemaphoreType.DMA((COPIES,)),
        ],
        compiler_params=pltpu.CompilerParams(
            collective_id=0, has_side_effects=True, vmem_limit_bytes=48 * 2**20
        ),
        cost_estimate=pl.CostEstimate(
            flops=3 * 8 * FULL * FULL * SHOTS, bytes_accessed=6 * 2**20, transcendentals=0
        ),
    )(sources, factor, block_mask, inverse_diagonal)


def solution(mesh):
    placed = (
        P("depth", None, "rows", "shots"),
        P("depth", None, ("rows", "shots"), None),
        P("depth", None, None, None),
        P("depth", None, None, "rows"),
    )
    return jax.shard_map(
        per_device,
        mesh=mesh,
        in_specs=placed,
        out_specs=P("depth", None, "rows", "shots"),
        check_vma=False,
    )
```

```python
import jax
import jax.numpy as jnp
from jax import lax
from jax.experimental import pallas as pl
from jax.experimental.pallas import tpu as pltpu
from jax.sharding import PartitionSpec as P

MESH = pl.DeviceIdType.MESH
F32 = jnp.float32
BF16 = jnp.bfloat16
BLOCK = 128
HALF = 512
FULL = 1024
SHOTS = 128


def split(x):
    high = x.astype(BF16)
    return high, (x - high.astype(F32)).astype(BF16)


def dot(a, b):
    return jnp.dot(a, b, preferred_element_type=F32)


def wide_product(a_high, a_low, b_pair):
    both = dot(a_high, b_pair)
    return both[:, :SHOTS] + both[:, SHOTS:] + dot(a_low, b_pair[:, :SHOTS])


def tall_product(a_pair, b_high, b_low):
    both = dot(a_pair, b_high)
    return both[:SHOTS] + both[SHOTS:] + dot(a_pair[:SHOTS], b_low)


class Copies:
    def __init__(self, send_sems, recv_sems):
        self.send_sems, self.recv_sems, self.count, self.sent = send_sems, recv_sems, 0, []

    def slot(self):
        self.count += 1
        return self.count - 1

    def make(self, slot, src, dst, device):
        return pltpu.make_async_remote_copy(
            src_ref=src,
            dst_ref=dst,
            send_sem=self.send_sems.at[slot],
            recv_sem=self.recv_sems.at[slot],
            device_id=device,
            device_id_type=MESH,
        )

    def send(self, slot, src, dst, device):
        copy = self.make(slot, src, dst, device)
        copy.start()
        self.sent.append(copy)

    def arrived(self, slot, dst, device):
        self.make(slot, dst, dst, device).wait_recv()

    def finish(self):
        for copy in self.sent:
            copy.wait_send()


COPIES = 104


def kernel(
    src_hbm,
    fac_hbm,
    mask_ref,
    inv_hbm,
    out_ref,
    src,
    fac,
    inv,
    tiles,
    tiles_high,
    tiles_low,
    inv_high,
    inv_low,
    low,
    low_in,
    low_pair,
    low_t,
    update,
    update_in,
    high_out,
    high_in,
    top_t,
    part_t,
    part_in,
    load_sems,
    send_sems,
    recv_sems,
):
    core = lax.axis_index("depth")
    row = lax.axis_index("rows")
    shot = lax.axis_index("shots")
    zy, xl = shot // 2, shot % 2
    z, y = zy // 4, zy % 4

    def at(dz, dy):
        return ((z + dz) % 4) * 4 + (y + dy) % 4

    def place(axis, step):
        return at(step, 0) if axis == 0 else at(0, step)

    def neighbour(axis, step):
        return (core, row, place(axis, step) * 2 + xl)

    beside = (core, row, zy * 2 + 1 - xl)
    across = (core, 1 - row, shot)
    twin = (1 - core, row, shot)

    loads = [
        pltpu.make_async_copy(fac_hbm.at[0], fac, load_sems.at[0]),
        pltpu.make_async_copy(src_hbm.at[0], src, load_sems.at[1]),
        pltpu.make_async_copy(inv_hbm.at[0, 0], inv.at[0], load_sems.at[2]),
        pltpu.make_async_copy(inv_hbm.at[0, 1], inv.at[1], load_sems.at[3]),
    ]
    for load in loads:
        load.start()

    barrier = pltpu.get_barrier_semaphore()
    partners = [neighbour(a, s) for a in (0, 1) for s in (1, -1)] + [beside, across, twin]
    for partner in partners:
        pl.semaphore_signal(barrier, inc=1, device_id=partner, device_id_type=MESH)

    loads[0].wait()
    row_block = row * 4 + zy // 4
    for t in range(2):
        for k in range(8):
            scale = mask_ref[0, t, row_block, k].astype(F32)
            piece = fac[t, :, k * BLOCK : (k + 1) * BLOCK] * scale
            tiles[t, k // 4, zy, xl, :, (k % 4) * BLOCK : (k % 4 + 1) * BLOCK] = piece

    pl.semaphore_wait(barrier, len(partners))

    copies = Copies(send_sems, recv_sems)
    parts = [(t, h) for t in range(2) for h in range(2)]
    first = {h: 1 - h for h in range(2)}
    slot_x = {p: copies.slot() for p in parts}
    slot_own = {(p, s): copies.slot() for p in parts for s in (1, -1)}
    slot_side = {(p, s): copies.slot() for p in parts for s in (1, -1)}
    slot_far = {(p, s): copies.slot() for p in parts for s in (1, -1)}
    units = (0, -1, 1, 2)
    slot_two = {(p, u, s): copies.slot() for p in parts for u in units for s in (1, -1)}
    slot_two_far = {(p, u, s): copies.slot() for p in parts for u in units for s in (1, -1)}
    slot_low = [copies.slot() for _ in range(2)]
    slot_update = copies.slot()
    slot_high = copies.slot()
    slot_top = copies.slot()
    slot_part = [copies.slot() for _ in range(4)]
    assert copies.count <= COPIES

    def unit_place(h, u, s):
        return at(s, u) if first[h] == 1 else at(u, s)

    def swap_beside(p):
        t, h = p
        piece = tiles.at[t, h, zy, xl]
        copies.send(slot_x[p], piece, piece, beside)

    def send_own(p):
        t, h = p
        piece = tiles.at[t, h, zy, xl]
        for s in (1, -1):
            copies.send(slot_own[p, s], piece, piece, neighbour(first[h], s))

    def wait_beside(p):
        t, h = p
        copies.arrived(slot_x[p], tiles.at[t, h, zy, 1 - xl], beside)

    def send_side(p):
        t, h = p
        piece = tiles.at[t, h, zy, 1 - xl]
        for s in (1, -1):
            copies.send(slot_side[p, s], piece, piece, neighbour(first[h], s))

    def send_unit(p, u):
        t, h = p
        piece = tiles.at[t, h, unit_place(h, u, 0)]
        for s in (1, -1):
            copies.send(slot_two[p, u, s], piece, piece, neighbour(1 - first[h], s))

    def relay_one(p, s):
        t, h = p
        where = unit_place(h, -s, 0)
        copies.arrived(slot_own[p, s], tiles.at[t, h, where, xl], neighbour(first[h], -s))
        copies.arrived(slot_side[p, s], tiles.at[t, h, where, 1 - xl], neighbour(first[h], -s))
        piece = tiles.at[t, h, where, 0 if s == 1 else 1]
        copies.send(slot_far[p, s], piece, piece, neighbour(first[h], s))

    def wait_far(p):
        t, h = p
        for s in (1, -1):
            piece = tiles.at[t, h, unit_place(h, 2, 0), 0 if s == 1 else 1]
            copies.arrived(slot_far[p, s], piece, neighbour(first[h], -s))

    def relay_two(p, u):
        t, h = p
        for s in (1, -1):
            where = unit_place(h, u, -s)
            copies.arrived(slot_two[p, u, s], tiles.at[t, h, where], neighbour(1 - first[h], -s))
            piece = tiles.at[t, h, where, 0 if s == 1 else 1]
            copies.send(slot_two_far[p, u, s], piece, piece, neighbour(1 - first[h], s))

    def wait_two_far(p, u):
        t, h = p
        for s in (1, -1):
            piece = tiles.at[t, h, unit_place(h, u, 2), 0 if s == 1 else 1]
            copies.arrived(slot_two_far[p, u, s], piece, neighbour(1 - first[h], -s))

    def pair(t):
        return [(t, 0), (t, 1)]

    def invert_split(m):
        loads[2 + m].wait()

        @pl.loop(0, 4)
        def _(i):
            rows = pl.ds(pl.multiple_of(i * 256, 256), 256)
            inv_high[m, rows], inv_low[m, rows] = split(inv[m, rows])

    bottom, upper = pl.ds(HALF, HALF), pl.ds(0, HALF)

    def low_share():
        source_pair = jnp.concatenate(split(src[0]), axis=1)

        @pl.loop(0, 4)
        def _(i):
            rows = pl.ds(pl.multiple_of(i * 256, 256), 256)
            low[rows] = wide_product(inv_high[0, rows], inv_low[0, rows], source_pair)

    def low_send():
        copies.send(slot_low[1], low.at[bottom], low_in.at[bottom], across)

        @pl.when(row == 0)
        def _():
            copies.make(slot_low[0], low.at[upper], low_in.at[upper], across).start()

    def low_sum():
        copies.arrived(slot_low[1], low_in.at[bottom], across)

        @pl.when(row == 1)
        def _():
            copies.arrived(slot_low[0], low_in.at[upper], across)

        @pl.when(row == 0)
        def _():
            low_in[upper] = low[upper]

        low_in[bottom] = low[bottom] + low_in[bottom]
        low_pair[...] = jnp.concatenate(split(low_in[...]), axis=1)
        low_t[...] = low_in[...].T

    def forward(t):
        @pl.loop(0, 4)
        def _(i):
            rows = pl.ds(pl.multiple_of(i * 128, 128), 128)
            total = jnp.zeros((128, SHOTS), F32)
            for h in range(2):
                block = tiles[t, h, pl.ds(i * 4, 4)].reshape(128, HALF)
                high, rest = split(block)
                cols = pl.ds(h * HALF, HALF)
                tiles_high[t, rows, cols] = high
                tiles_low[t, rows, cols] = rest
                total += wide_product(high, rest, low_pair[cols])
            update[t, rows] = total

        @pl.when(core != t)
        def _():
            copies.make(slot_update, update.at[t], update_in, twin).start()

    high_copy = copies.make(slot_high, high_out.at[bottom], high_in, across)

    def level_one_down(t):
        @pl.when(core == t)
        def _():
            copies.arrived(slot_update, update_in, twin)
            own_pair = jnp.concatenate(split(src[1] - update[t] - update_in[...]), axis=1)

            @pl.loop(0, 4)
            def _(i):
                rows = pl.ds(pl.multiple_of(i * 256, 256), 256)
                high_out[rows] = wide_product(inv_high[1, rows], inv_low[1, rows], own_pair)

            high_copy.start()

    def level_one_up(t):
        @pl.when(core == t)
        def _():
            upper_pair = jnp.concatenate(split(high_out[upper].T), axis=0)
            total = tall_product(upper_pair, inv_high[1, upper], inv_low[1, upper])
            high_copy.wait()
            lower_pair = jnp.concatenate(split((high_out[bottom] + high_in[...]).T), axis=0)
            total += tall_product(lower_pair, inv_high[1, bottom], inv_low[1, bottom])
            top_t[t] = total
            copies.make(slot_top, top_t.at[t], top_t.at[t], twin).start()
            out_ref[0, 1] = total.T

    def backward(t):
        @pl.when(core != t)
        def _():
            copies.arrived(slot_top, top_t.at[t], twin)

        top_pair = jnp.concatenate(split(top_t[t]), axis=0)
        for k in range(4):
            cols = pl.ds(k * 256, 256)
            share = tall_product(top_pair, tiles_high[t, :, cols], tiles_low[t, :, cols])
            part_t[k] = share if t == 0 else part_t[k] + share

    def each(t, step, *rest):
        for p in pair(t):
            step(p, *rest)

    each(0, swap_beside)
    each(0, send_own)
    each(1, swap_beside)
    loads[1].wait()
    invert_split(0)
    low_share()
    each(0, wait_beside)
    each(0, send_side)
    each(0, send_unit, 0)
    low_send()
    each(1, send_own)
    each(1, wait_beside)
    each(1, send_side)
    for s in (1, -1):
        each(0, relay_one, s)
    for s in (1, -1):
        each(0, send_unit, s)
    each(0, relay_two, 0)
    each(0, wait_far)
    each(0, send_unit, 2)
    each(1, send_unit, 0)
    invert_split(1)
    for s in (1, -1):
        each(0, relay_two, s)
    for s in (1, -1):
        each(1, relay_one, s)
    each(0, relay_two, 2)
    for s in (1, -1):
        each(1, send_unit, s)
    each(1, relay_two, 0)
    low_sum()
    each(1, wait_far)
    each(1, send_unit, 2)
    for u in units:
        each(0, wait_two_far, u)
    forward(0)
    for s in (1, -1):
        each(1, relay_two, s)
    level_one_down(0)
    each(1, relay_two, 2)
    for u in units:
        each(1, wait_two_far, u)
    forward(1)
    level_one_down(1)
    level_one_up(0)
    backward(0)
    level_one_up(1)
    backward(1)

    for k in (2, 3):
        copies.send(slot_part[k], part_t.at[k], part_in.at[k], across)

    @pl.when(row == 1)
    def _():
        for k in (0, 1):
            copies.make(slot_part[k], part_t.at[k], part_in.at[k], across).start()

    def final(k):
        cols = pl.ds(k * 256, 256)
        copies.arrived(slot_part[k], part_in.at[k], across)
        target = low_t[:, cols] - part_t[k] - part_in[k]
        pair_ = jnp.concatenate(split(target), axis=0)
        return tall_product(pair_, inv_high[0, cols], inv_low[0, cols])

    answer = final(2) + final(3)
    low_in[pl.ds(0, HALF)] = answer.T

    @pl.when(row == 0)
    def _():
        more = final(0) + final(1)
        low_in[pl.ds(0, HALF)] = low_in[pl.ds(0, HALF)] + more.T

    out_ref[0, 0] = low_in[pl.ds(0, HALF)]

    copies.finish()
    for t in range(2):

        @pl.when(core == t)
        def _():
            copies.make(slot_update, update.at[1 - t], update_in, twin).wait_send()
            copies.make(slot_top, top_t.at[t], top_t.at[t], twin).wait_send()

    @pl.when(row == 0)
    def _():
        copies.make(slot_low[0], low.at[upper], low_in.at[upper], across).wait_send()

    @pl.when(row == 1)
    def _():
        for k in (0, 1):
            copies.make(slot_part[k], part_t.at[k], part_in.at[k], across).wait_send()


def per_device(sources, factor, block_mask, inverse_diagonal):
    return pl.pallas_call(
        kernel,
        out_shape=jax.ShapeDtypeStruct(sources.shape, F32),
        in_specs=[
            pl.BlockSpec(memory_space=pltpu.HBM),
            pl.BlockSpec(memory_space=pltpu.HBM),
            pl.BlockSpec(memory_space=pltpu.SMEM),
            pl.BlockSpec(memory_space=pltpu.HBM),
        ],
        out_specs=pl.BlockSpec(memory_space=pltpu.VMEM),
        scratch_shapes=[
            pltpu.VMEM((2, HALF, SHOTS), F32),
            pltpu.VMEM((2, 16, FULL), F32),
            pltpu.VMEM((2, FULL, HALF), F32),
            pltpu.VMEM((2, 2, 16, 2, 16, HALF), F32),
            pltpu.VMEM((2, HALF, FULL), BF16),
            pltpu.VMEM((2, HALF, FULL), BF16),
            pltpu.VMEM((2, FULL, HALF), BF16),
            pltpu.VMEM((2, FULL, HALF), BF16),
            pltpu.VMEM((FULL, SHOTS), F32),
            pltpu.VMEM((FULL, SHOTS), F32),
            pltpu.VMEM((FULL, 2 * SHOTS), BF16),
            pltpu.VMEM((SHOTS, FULL), F32),
            pltpu.VMEM((2, HALF, SHOTS), F32),
            pltpu.VMEM((HALF, SHOTS), F32),
            pltpu.VMEM((FULL, SHOTS), F32),
            pltpu.VMEM((HALF, SHOTS), F32),
            pltpu.VMEM((2, SHOTS, HALF), F32),
            pltpu.VMEM((4, SHOTS, 256), F32),
            pltpu.VMEM((4, SHOTS, 256), F32),
            pltpu.SemaphoreType.DMA((4,)),
            pltpu.SemaphoreType.DMA((COPIES,)),
            pltpu.SemaphoreType.DMA((COPIES,)),
        ],
        compiler_params=pltpu.CompilerParams(
            collective_id=0, has_side_effects=True, vmem_limit_bytes=60 * 2**20
        ),
        cost_estimate=pl.CostEstimate(
            flops=3 * 8 * FULL * FULL * SHOTS, bytes_accessed=6 * 2**20, transcendentals=0
        ),
    )(sources, factor, block_mask, inverse_diagonal)


def solution(mesh):
    placed = (
        P("depth", None, "rows", "shots"),
        P("depth", None, ("rows", "shots"), None),
        P("depth", None, None, None),
        P("depth", None, None, "rows"),
    )
    return jax.shard_map(
        per_device,
        mesh=mesh,
        in_specs=placed,
        out_specs=P("depth", None, "rows", "shots"),
        check_vma=False,
    )
```

```python
import jax
import jax.numpy as jnp
from jax import lax
from jax.experimental import pallas as pl
from jax.experimental.pallas import tpu as pltpu
from jax.sharding import PartitionSpec as P

MESH = pl.DeviceIdType.MESH
F32 = jnp.float32
BF16 = jnp.bfloat16
BLOCK = 128
HALF = 512
FULL = 1024
SHOTS = 128


def split(x):
    high = x.astype(BF16)
    return high, (x - high.astype(F32)).astype(BF16)


def dot(a, b):
    return jnp.dot(a, b, preferred_element_type=F32)


def wide_product(a_high, a_low, b_pair):
    both = dot(a_high, b_pair)
    return both[:, :SHOTS] + both[:, SHOTS:] + dot(a_low, b_pair[:, :SHOTS])


def tall_product(a_pair, b_high, b_low):
    both = dot(a_pair, b_high)
    return both[:SHOTS] + both[SHOTS:] + dot(a_pair[:SHOTS], b_low)


class Copies:
    def __init__(self, send_sems, recv_sems):
        self.send_sems, self.recv_sems, self.count, self.sent = send_sems, recv_sems, 0, []

    def slot(self):
        self.count += 1
        return self.count - 1

    def make(self, slot, src, dst, device):
        return pltpu.make_async_remote_copy(
            src_ref=src,
            dst_ref=dst,
            send_sem=self.send_sems.at[slot],
            recv_sem=self.recv_sems.at[slot],
            device_id=device,
            device_id_type=MESH,
        )

    def send(self, slot, src, dst, device):
        copy = self.make(slot, src, dst, device)
        copy.start()
        self.sent.append(copy)

    def arrived(self, slot, dst, device):
        self.make(slot, dst, dst, device).wait_recv()

    def finish(self):
        for copy in self.sent:
            copy.wait_send()


COPIES = 112


def kernel(
    src_hbm,
    fac_hbm,
    mask_ref,
    inv_hbm,
    out_ref,
    src,
    fac,
    inv,
    tiles,
    tiles_high,
    tiles_low,
    inv_high,
    inv_low,
    low,
    low_in,
    low_pair,
    low_t,
    update,
    update_in,
    high_out,
    high_in,
    top_t,
    part_t,
    part_in,
    answer_t,
    answers,
    load_sems,
    send_sems,
    recv_sems,
):
    core = lax.axis_index("depth")
    row = lax.axis_index("rows")
    shot = lax.axis_index("shots")
    zy, xl = shot // 2, shot % 2
    z, y = zy // 4, zy % 4

    def at(dz, dy):
        return ((z + dz) % 4) * 4 + (y + dy) % 4

    def place(axis, step):
        return at(step, 0) if axis == 0 else at(0, step)

    def neighbour(axis, step):
        return (core, row, place(axis, step) * 2 + xl)

    beside = (core, row, zy * 2 + 1 - xl)
    across = (core, 1 - row, shot)
    twin = (1 - core, row, shot)

    loads = [
        pltpu.make_async_copy(fac_hbm.at[0], fac, load_sems.at[0]),
        pltpu.make_async_copy(src_hbm.at[0], src, load_sems.at[1]),
        pltpu.make_async_copy(inv_hbm.at[0, 0], inv.at[0], load_sems.at[2]),
        pltpu.make_async_copy(inv_hbm.at[0, 1], inv.at[1], load_sems.at[3]),
    ]
    for load in loads:
        load.start()

    barrier = pltpu.get_barrier_semaphore()
    partners = [neighbour(a, s) for a in (0, 1) for s in (1, -1)] + [beside, across, twin]
    for partner in partners:
        pl.semaphore_signal(barrier, inc=1, device_id=partner, device_id_type=MESH)

    def invert_split(m):
        loads[2 + m].wait()

        @pl.loop(0, 4)
        def _(i):
            rows = pl.ds(pl.multiple_of(i * 256, 256), 256)
            inv_high[m, rows], inv_low[m, rows] = split(inv[m, rows])

    def write_out(m):
        return pltpu.make_async_copy(answers.at[m], out_ref.at[0, m], load_sems.at[4 + m])

    loads[0].wait()
    row_block = row * 4 + zy // 4
    for t in range(2):
        for k in range(8):
            scale = mask_ref[0, t, row_block, k].astype(F32)
            piece = fac[t, :, k * BLOCK : (k + 1) * BLOCK] * scale
            tiles[t, k // 4, zy, xl, :, (k % 4) * BLOCK : (k % 4 + 1) * BLOCK] = piece

    invert_split(0)
    pl.semaphore_wait(barrier, len(partners))

    copies = Copies(send_sems, recv_sems)
    parts = [(t, h) for t in range(2) for h in range(2)]
    first = {h: 1 - h for h in range(2)}
    slot_x = {p: copies.slot() for p in parts}
    slot_own = {(p, s): copies.slot() for p in parts for s in (1, -1)}
    slot_side = {(p, s): copies.slot() for p in parts for s in (1, -1)}
    slot_far = {(p, s): copies.slot() for p in parts for s in (1, -1)}
    units = (0, -1, 1, 2)
    slot_two = {(p, u, s): copies.slot() for p in parts for u in units for s in (1, -1)}
    slot_two_far = {(p, u, s): copies.slot() for p in parts for u in units for s in (1, -1)}
    slot_low = [copies.slot() for _ in range(2)]
    slot_update = [copies.slot() for _ in range(4)]
    slot_high = [copies.slot() for _ in range(2)]
    slot_top = [copies.slot() for _ in range(2)]
    slot_part = [copies.slot() for _ in range(4)]
    assert copies.count <= COPIES

    def unit_place(h, u, s):
        return at(s, u) if first[h] == 1 else at(u, s)

    def swap_beside(p):
        t, h = p
        piece = tiles.at[t, h, zy, xl]
        copies.send(slot_x[p], piece, piece, beside)

    def send_own(p):
        t, h = p
        piece = tiles.at[t, h, zy, xl]
        for s in (1, -1):
            copies.send(slot_own[p, s], piece, piece, neighbour(first[h], s))

    def wait_beside(p):
        t, h = p
        copies.arrived(slot_x[p], tiles.at[t, h, zy, 1 - xl], beside)

    def send_side(p):
        t, h = p
        piece = tiles.at[t, h, zy, 1 - xl]
        for s in (1, -1):
            copies.send(slot_side[p, s], piece, piece, neighbour(first[h], s))

    def send_unit(p, u):
        t, h = p
        piece = tiles.at[t, h, unit_place(h, u, 0)]
        for s in (1, -1):
            copies.send(slot_two[p, u, s], piece, piece, neighbour(1 - first[h], s))

    def relay_one(p, s):
        t, h = p
        where = unit_place(h, -s, 0)
        copies.arrived(slot_own[p, s], tiles.at[t, h, where, xl], neighbour(first[h], -s))
        copies.arrived(slot_side[p, s], tiles.at[t, h, where, 1 - xl], neighbour(first[h], -s))
        piece = tiles.at[t, h, where, 0 if s == 1 else 1]
        copies.send(slot_far[p, s], piece, piece, neighbour(first[h], s))

    def wait_far(p):
        t, h = p
        for s in (1, -1):
            piece = tiles.at[t, h, unit_place(h, 2, 0), 0 if s == 1 else 1]
            copies.arrived(slot_far[p, s], piece, neighbour(first[h], -s))

    def relay_two(p, u):
        t, h = p
        for s in (1, -1):
            where = unit_place(h, u, -s)
            copies.arrived(slot_two[p, u, s], tiles.at[t, h, where], neighbour(1 - first[h], -s))
            piece = tiles.at[t, h, where, 0 if s == 1 else 1]
            copies.send(slot_two_far[p, u, s], piece, piece, neighbour(1 - first[h], s))

    def wait_two_far(p, u):
        t, h = p
        for s in (1, -1):
            piece = tiles.at[t, h, unit_place(h, u, 2), 0 if s == 1 else 1]
            copies.arrived(slot_two_far[p, u, s], piece, neighbour(1 - first[h], -s))

    def pair(t):
        return [(t, 0), (t, 1)]

    bottom, upper = pl.ds(HALF, HALF), pl.ds(0, HALF)

    def low_share():
        source_pair = jnp.concatenate(split(src[0]), axis=1)

        @pl.loop(0, 4)
        def _(i):
            rows = pl.ds(pl.multiple_of(i * 256, 256), 256)
            low[rows] = wide_product(inv_high[0, rows], inv_low[0, rows], source_pair)

    def low_send():
        copies.send(slot_low[1], low.at[bottom], low_in.at[bottom], across)

        @pl.when(row == 0)
        def _():
            copies.make(slot_low[0], low.at[upper], low_in.at[upper], across).start()

    def low_sum():
        copies.arrived(slot_low[1], low_in.at[bottom], across)

        @pl.when(row == 1)
        def _():
            copies.arrived(slot_low[0], low_in.at[upper], across)

        @pl.when(row == 0)
        def _():
            low_in[upper] = low[upper]

        low_in[bottom] = low[bottom] + low_in[bottom]
        low_pair[...] = jnp.concatenate(split(low_in[...]), axis=1)

    def update_copy(t, i):
        rows = pl.ds(i * 128, 128)
        return copies.make(slot_update[i], update.at[t, rows], update_in.at[rows], twin)

    def forward(t, chunks):
        for i in chunks:
            rows = pl.ds(i * 128, 128)
            total = jnp.zeros((128, SHOTS), F32)
            for h in range(2):
                block = tiles[t, h, pl.ds(i * 4, 4)].reshape(128, HALF)
                high, rest = split(block)
                cols = pl.ds(h * HALF, HALF)
                tiles_high[t, rows, cols] = high
                tiles_low[t, rows, cols] = rest
                total += wide_product(high, rest, low_pair[cols])
            update[t, rows] = total

            @pl.when(core != t)
            def _():
                update_copy(t, i).start()

    def high_copy(i):
        rows = pl.ds(HALF + i * 256, 256)
        return copies.make(slot_high[i], high_out.at[rows], high_in.at[pl.ds(i * 256, 256)], across)

    def level_one_down(t):
        @pl.when(core == t)
        def _():
            for i in range(4):
                update_copy(t, i).wait_recv()
            own_pair = jnp.concatenate(split(src[1] - update[t] - update_in[...]), axis=1)
            for i in (2, 3, 0, 1):
                rows = pl.ds(i * 256, 256)
                high_out[rows] = wide_product(inv_high[1, rows], inv_low[1, rows], own_pair)
                if i >= 2:
                    high_copy(i - 2).start()

    def top_copy(t, i):
        return copies.make(slot_top[i], top_t.at[t, i], top_t.at[t, i], twin)

    def level_one_up(t):
        @pl.when(core == t)
        def _():
            upper_pair = jnp.concatenate(split(high_out[upper].T), axis=0)
            halves = [pl.ds(i * 256, 256) for i in range(2)]
            for i in range(2):
                top_t[t, i] = tall_product(upper_pair, inv_high[1, upper, halves[i]], inv_low[1, upper, halves[i]])
            for i in range(2):
                high_copy(i).wait()
            lower_pair = jnp.concatenate(split((high_out[bottom] + high_in[...]).T), axis=0)
            for i in range(2):
                top_t[t, i] = top_t[t, i] + tall_product(
                    lower_pair, inv_high[1, bottom, halves[i]], inv_low[1, bottom, halves[i]]
                )
                top_copy(t, i).start()

    def top_out(t):
        @pl.when(core == t)
        def _():
            for i in range(2):
                answers[1, pl.ds(i * 256, 256)] = top_t[t, i].T
            write_out(1).start()

    def part_copy(k):
        return copies.make(slot_part[k], part_t.at[k], part_in.at[k], across)

    def backward(t):
        @pl.when(core != t)
        def _():
            for i in range(2):
                top_copy(t, i).wait_recv()

        top_pair = jnp.concatenate(split(jnp.concatenate([top_t[t, 0], top_t[t, 1]], axis=1)), axis=0)
        for k in (2, 3, 0, 1):
            cols = pl.ds(k * 256, 256)
            share = tall_product(top_pair, tiles_high[t, :, cols], tiles_low[t, :, cols])
            part_t[k] = share if t == 0 else part_t[k] + share
            if t == 1 and k >= 2:
                copies.send(slot_part[k], part_t.at[k], part_in.at[k], across)
            elif t == 1:

                @pl.when(row == 1)
                def _():
                    part_copy(k).start()

    def each(t, step, *rest):
        for p in pair(t):
            step(p, *rest)

    each(0, swap_beside)
    each(0, send_own)
    each(1, swap_beside)
    loads[1].wait()
    low_share()
    each(0, wait_beside)
    each(0, send_side)
    each(0, send_unit, 0)
    low_send()
    each(1, send_own)
    each(1, wait_beside)
    each(1, send_side)
    for s in (1, -1):
        each(0, relay_one, s)
    for s in (1, -1):
        each(0, send_unit, s)
    each(0, relay_two, 0)
    each(0, wait_far)
    each(0, send_unit, 2)
    each(1, send_unit, 0)
    invert_split(1)
    for s in (1, -1):
        each(0, relay_two, s)
    for s in (1, -1):
        each(1, relay_one, s)
    each(0, relay_two, 2)
    for s in (1, -1):
        each(1, send_unit, s)
    each(1, relay_two, 0)
    low_sum()
    each(1, wait_far)
    each(1, send_unit, 2)
    for u in units:
        each(0, wait_two_far, u)
    forward(0, (0, 1))
    each(1, relay_two, 1)
    forward(0, (2, 3))
    each(1, relay_two, -1)
    level_one_down(0)
    each(1, relay_two, 2)
    for u in units:
        each(1, wait_two_far, u)
    forward(1, range(4))
    level_one_down(1)
    level_one_up(0)
    top_out(0)
    backward(0)
    low_t[...] = low_in[...].T
    level_one_up(1)
    backward(1)
    top_out(1)

    def final(k):
        cols = pl.ds(k * 256, 256)
        copies.arrived(slot_part[k], part_in.at[k], across)
        target = low_t[:, cols] - part_t[k] - part_in[k]
        pair_ = jnp.concatenate(split(target), axis=0)
        return tall_product(pair_, inv_high[0, cols], inv_low[0, cols])

    answer_t[...] = final(2) + final(3)

    @pl.when(row == 0)
    def _():
        answer_t[...] = answer_t[...] + final(0)
        answer_t[...] = answer_t[...] + final(1)

    answers[0] = answer_t[...].T
    write_out(0).start()

    copies.finish()
    for t in range(2):

        @pl.when(core == t)
        def _():
            for i in range(4):
                update_copy(1 - t, i).wait_send()
            for i in range(2):
                top_copy(t, i).wait_send()

    @pl.when(row == 0)
    def _():
        copies.make(slot_low[0], low.at[upper], low_in.at[upper], across).wait_send()

    @pl.when(row == 1)
    def _():
        for k in (0, 1):
            part_copy(k).wait_send()

    for m in range(2):
        write_out(m).wait()


def per_device(sources, factor, block_mask, inverse_diagonal):
    return pl.pallas_call(
        kernel,
        out_shape=jax.ShapeDtypeStruct(sources.shape, F32),
        in_specs=[
            pl.BlockSpec(memory_space=pltpu.HBM),
            pl.BlockSpec(memory_space=pltpu.HBM),
            pl.BlockSpec(memory_space=pltpu.SMEM),
            pl.BlockSpec(memory_space=pltpu.HBM),
        ],
        out_specs=pl.BlockSpec(memory_space=pltpu.HBM),
        scratch_shapes=[
            pltpu.VMEM((2, HALF, SHOTS), F32),
            pltpu.VMEM((2, 16, FULL), F32),
            pltpu.VMEM((2, FULL, HALF), F32),
            pltpu.VMEM((2, 2, 16, 2, 16, HALF), F32),
            pltpu.VMEM((2, HALF, FULL), BF16),
            pltpu.VMEM((2, HALF, FULL), BF16),
            pltpu.VMEM((2, FULL, HALF), BF16),
            pltpu.VMEM((2, FULL, HALF), BF16),
            pltpu.VMEM((FULL, SHOTS), F32),
            pltpu.VMEM((FULL, SHOTS), F32),
            pltpu.VMEM((FULL, 2 * SHOTS), BF16),
            pltpu.VMEM((SHOTS, FULL), F32),
            pltpu.VMEM((2, HALF, SHOTS), F32),
            pltpu.VMEM((HALF, SHOTS), F32),
            pltpu.VMEM((FULL, SHOTS), F32),
            pltpu.VMEM((HALF, SHOTS), F32),
            pltpu.VMEM((2, 2, SHOTS, 256), F32),
            pltpu.VMEM((4, SHOTS, 256), F32),
            pltpu.VMEM((4, SHOTS, 256), F32),
            pltpu.VMEM((SHOTS, HALF), F32),
            pltpu.VMEM((2, HALF, SHOTS), F32),
            pltpu.SemaphoreType.DMA((6,)),
            pltpu.SemaphoreType.DMA((COPIES,)),
            pltpu.SemaphoreType.DMA((COPIES,)),
        ],
        compiler_params=pltpu.CompilerParams(
            collective_id=0, has_side_effects=True, vmem_limit_bytes=60 * 2**20
        ),
        cost_estimate=pl.CostEstimate(
            flops=3 * 8 * FULL * FULL * SHOTS, bytes_accessed=6 * 2**20, transcendentals=0
        ),
    )(sources, factor, block_mask, inverse_diagonal)


def solution(mesh):
    placed = (
        P("depth", None, "rows", "shots"),
        P("depth", None, ("rows", "shots"), None),
        P("depth", None, None, None),
        P("depth", None, None, "rows"),
    )
    return jax.shard_map(
        per_device,
        mesh=mesh,
        in_specs=placed,
        out_specs=P("depth", None, "rows", "shots"),
        check_vma=False,
    )
```

```python
import jax
import jax.numpy as jnp
from jax import lax
from jax.experimental import pallas as pl
from jax.experimental.pallas import tpu as pltpu
from jax.sharding import PartitionSpec as P

MESH = pl.DeviceIdType.MESH
F32 = jnp.float32
BF16 = jnp.bfloat16
BLOCK = 128
DIRECT = (0, 1)
HALF = 512
FULL = 1024
SHOTS = 128


def split(x):
    high = x.astype(BF16)
    return high, (x - high.astype(F32)).astype(BF16)


def dot(a, b):
    return jnp.dot(a, b, preferred_element_type=F32)


def wide_product(a_high, a_low, b_pair):
    both = dot(a_high, b_pair)
    return both[:, :SHOTS] + both[:, SHOTS:] + dot(a_low, b_pair[:, :SHOTS])


def tall_product(a_pair, b_high, b_low):
    both = dot(a_pair, b_high)
    return both[:SHOTS] + both[SHOTS:] + dot(a_pair[:SHOTS], b_low)


class Copies:
    def __init__(self, send_sems, recv_sems):
        self.send_sems, self.recv_sems, self.count, self.sent = send_sems, recv_sems, 0, []

    def slot(self):
        self.count += 1
        return self.count - 1

    def make(self, slot, src, dst, device):
        return pltpu.make_async_remote_copy(
            src_ref=src,
            dst_ref=dst,
            send_sem=self.send_sems.at[slot],
            recv_sem=self.recv_sems.at[slot],
            device_id=device,
            device_id_type=MESH,
        )

    def send(self, slot, src, dst, device):
        copy = self.make(slot, src, dst, device)
        copy.start()
        self.sent.append(copy)

    def arrived(self, slot, dst, device):
        self.make(slot, dst, dst, device).wait_recv()

    def finish(self):
        for copy in self.sent:
            copy.wait_send()


COPIES = 112


def kernel(
    src_hbm,
    fac_hbm,
    mask_ref,
    inv_hbm,
    out_ref,
    src,
    fac,
    inv,
    tiles,
    tiles_high,
    tiles_low,
    inv_high,
    inv_low,
    low,
    low_in,
    low_pair,
    low_t,
    update,
    update_in,
    high_out,
    high_in,
    top_t,
    part_t,
    part_in,
    answer_t,
    answers,
    load_sems,
    send_sems,
    recv_sems,
):
    core = lax.axis_index("depth")
    row = lax.axis_index("rows")
    shot = lax.axis_index("shots")
    zy, xl = shot // 2, shot % 2
    z, y = zy // 4, zy % 4

    def at(dz, dy):
        return ((z + dz) % 4) * 4 + (y + dy) % 4

    def place(axis, step):
        return at(step, 0) if axis == 0 else at(0, step)

    def neighbour(axis, step):
        return (core, row, place(axis, step) * 2 + xl)

    beside = (core, row, zy * 2 + 1 - xl)
    across = (core, 1 - row, shot)
    twin = (1 - core, row, shot)

    loads = [
        pltpu.make_async_copy(fac_hbm.at[0], fac, load_sems.at[0]),
        pltpu.make_async_copy(src_hbm.at[0], src, load_sems.at[1]),
        pltpu.make_async_copy(inv_hbm.at[0, 0], inv.at[0], load_sems.at[2]),
        pltpu.make_async_copy(inv_hbm.at[0, 1], inv.at[1], load_sems.at[3]),
    ]
    for load in loads:
        load.start()

    barrier = pltpu.get_barrier_semaphore()
    partners = [neighbour(a, s) for a in (0, 1) for s in (1, -1)] + [beside, across, twin, neighbour(0, 2), neighbour(1, 2)]
    for partner in partners:
        pl.semaphore_signal(barrier, inc=1, device_id=partner, device_id_type=MESH)

    def invert_split(m):
        loads[2 + m].wait()

        @pl.loop(0, 4)
        def _(i):
            rows = pl.ds(pl.multiple_of(i * 256, 256), 256)
            inv_high[m, rows], inv_low[m, rows] = split(inv[m, rows])

    def write_out(m):
        return pltpu.make_async_copy(answers.at[m], out_ref.at[0, m], load_sems.at[4 + m])

    loads[0].wait()
    row_block = row * 4 + zy // 4
    for t in range(2):
        for k in range(8):
            scale = mask_ref[0, t, row_block, k].astype(F32)
            piece = fac[t, :, k * BLOCK : (k + 1) * BLOCK] * scale
            tiles[t, k // 4, zy, xl, :, (k % 4) * BLOCK : (k % 4 + 1) * BLOCK] = piece

    invert_split(0)
    pl.semaphore_wait(barrier, len(partners))

    copies = Copies(send_sems, recv_sems)
    parts = [(t, h) for t in range(2) for h in range(2)]
    first = {h: 1 - h for h in range(2)}
    slot_x = {p: copies.slot() for p in parts}
    slot_own = {(p, s): copies.slot() for p in parts for s in (1, -1)}
    slot_side = {(p, s): copies.slot() for p in parts for s in (1, -1)}
    slot_far = {(p, s): copies.slot() for p in parts for s in (1, -1)}
    units = (0, -1, 1, 2)
    slot_two = {(p, u, s): copies.slot() for p in parts for u in units for s in (1, -1)}
    slot_two_far = {(p, u, s): copies.slot() for p in parts for u in units for s in (1, -1)}
    slot_low = [copies.slot() for _ in range(2)]
    slot_update = [copies.slot() for _ in range(4)]
    slot_high = [copies.slot() for _ in range(2)]
    slot_top = [copies.slot() for _ in range(2)]
    slot_part = [copies.slot() for _ in range(4)]
    assert copies.count <= COPIES

    def unit_place(h, u, s):
        return at(s, u) if first[h] == 1 else at(u, s)

    def swap_beside(p):
        t, h = p
        piece = tiles.at[t, h, zy, xl]
        copies.send(slot_x[p], piece, piece, beside)

    def send_own(p):
        t, h = p
        piece = tiles.at[t, h, zy, xl]
        for s in (1, -1):
            copies.send(slot_own[p, s], piece, piece, neighbour(first[h], s))
        if t in DIRECT:
            copies.send(slot_far[p, 1], piece, piece, neighbour(first[h], 2))

    def wait_beside(p):
        t, h = p
        copies.arrived(slot_x[p], tiles.at[t, h, zy, 1 - xl], beside)

    def send_side(p):
        t, h = p
        piece = tiles.at[t, h, zy, 1 - xl]
        for s in (1, -1):
            copies.send(slot_side[p, s], piece, piece, neighbour(first[h], s))
        if t in DIRECT:
            copies.send(slot_far[p, -1], piece, piece, neighbour(first[h], 2))

    def send_unit(p, u):
        t, h = p
        piece = tiles.at[t, h, unit_place(h, u, 0)]
        for s in (1, -1):
            copies.send(slot_two[p, u, s], piece, piece, neighbour(1 - first[h], s))
        if t == 1 and u == 2:
            copies.send(slot_two_far[p, u, 1], piece, piece, neighbour(1 - first[h], 2))

    def relay_one(p, s):
        t, h = p
        where = unit_place(h, -s, 0)
        copies.arrived(slot_own[p, s], tiles.at[t, h, where, xl], neighbour(first[h], -s))
        copies.arrived(slot_side[p, s], tiles.at[t, h, where, 1 - xl], neighbour(first[h], -s))
        if t not in DIRECT:
            piece = tiles.at[t, h, where, 0 if s == 1 else 1]
            copies.send(slot_far[p, s], piece, piece, neighbour(first[h], s))

    def wait_far(p):
        t, h = p
        for s in (1, -1):
            which = 0 if s == 1 else 1
            if t in DIRECT:
                which = xl if s == 1 else 1 - xl
            piece = tiles.at[t, h, unit_place(h, 2, 0), which]
            copies.arrived(slot_far[p, s], piece, neighbour(first[h], 2))

    def relay_two(p, u):
        t, h = p
        for s in (1, -1):
            where = unit_place(h, u, -s)
            copies.arrived(slot_two[p, u, s], tiles.at[t, h, where], neighbour(1 - first[h], -s))
            if t == 1 and u == 2:
                continue
            piece = tiles.at[t, h, where, 0 if s == 1 else 1]
            copies.send(slot_two_far[p, u, s], piece, piece, neighbour(1 - first[h], s))

    def wait_two_far(p, u):
        t, h = p
        if t == 1 and u == 2:
            copies.arrived(slot_two_far[p, u, 1], tiles.at[t, h, unit_place(h, u, 2)], neighbour(1 - first[h], 2))
            return
        for s in (1, -1):
            piece = tiles.at[t, h, unit_place(h, u, 2), 0 if s == 1 else 1]
            copies.arrived(slot_two_far[p, u, s], piece, neighbour(1 - first[h], -s))

    def pair(t):
        return [(t, 0), (t, 1)]

    bottom, upper = pl.ds(HALF, HALF), pl.ds(0, HALF)

    def low_share():
        source_pair = jnp.concatenate(split(src[0]), axis=1)

        @pl.loop(0, 4)
        def _(i):
            rows = pl.ds(pl.multiple_of(i * 256, 256), 256)
            low[rows] = wide_product(inv_high[0, rows], inv_low[0, rows], source_pair)

    def low_send():
        copies.send(slot_low[1], low.at[bottom], low_in.at[bottom], across)

        @pl.when(row == 0)
        def _():
            copies.make(slot_low[0], low.at[upper], low_in.at[upper], across).start()

    def low_sum():
        copies.arrived(slot_low[1], low_in.at[bottom], across)

        @pl.when(row == 1)
        def _():
            copies.arrived(slot_low[0], low_in.at[upper], across)

        @pl.when(row == 0)
        def _():
            low_in[upper] = low[upper]

        low_in[bottom] = low[bottom] + low_in[bottom]
        low_pair[...] = jnp.concatenate(split(low_in[...]), axis=1)

    def update_copy(t, i):
        rows = pl.ds(i * 128, 128)
        return copies.make(slot_update[i], update.at[t, rows], update_in.at[rows], twin)

    def forward(t, chunks):
        for i in chunks:
            rows = pl.ds(i * 128, 128)
            total = jnp.zeros((128, SHOTS), F32)
            for h in range(2):
                block = tiles[t, h, pl.ds(i * 4, 4)].reshape(128, HALF)
                high, rest = split(block)
                cols = pl.ds(h * HALF, HALF)
                tiles_high[t, rows, cols] = high
                tiles_low[t, rows, cols] = rest
                total += wide_product(high, rest, low_pair[cols])
            update[t, rows] = total

            @pl.when(core != t)
            def _():
                update_copy(t, i).start()

    def high_copy(i):
        rows = pl.ds(HALF + i * 256, 256)
        return copies.make(slot_high[i], high_out.at[rows], high_in.at[pl.ds(i * 256, 256)], across)

    def level_one_down(t):
        @pl.when(core == t)
        def _():
            for i in range(4):
                update_copy(t, i).wait_recv()
            own_pair = jnp.concatenate(split(src[1] - update[t] - update_in[...]), axis=1)
            for i in (2, 3, 0, 1):
                rows = pl.ds(i * 256, 256)
                high_out[rows] = wide_product(inv_high[1, rows], inv_low[1, rows], own_pair)
                if i >= 2:
                    high_copy(i - 2).start()

    def top_copy(t, i):
        return copies.make(slot_top[i], top_t.at[t, i], top_t.at[t, i], twin)

    def level_one_up(t):
        @pl.when(core == t)
        def _():
            upper_pair = jnp.concatenate(split(high_out[upper].T), axis=0)
            halves = [pl.ds(i * 256, 256) for i in range(2)]
            for i in range(2):
                top_t[t, i] = tall_product(upper_pair, inv_high[1, upper, halves[i]], inv_low[1, upper, halves[i]])
            for i in range(2):
                high_copy(i).wait()
            lower_pair = jnp.concatenate(split((high_out[bottom] + high_in[...]).T), axis=0)
            for i in range(2):
                top_t[t, i] = top_t[t, i] + tall_product(
                    lower_pair, inv_high[1, bottom, halves[i]], inv_low[1, bottom, halves[i]]
                )
                top_copy(t, i).start()

    def top_out(t):
        @pl.when(core == t)
        def _():
            for i in range(2):
                answers[1, pl.ds(i * 256, 256)] = top_t[t, i].T
            write_out(1).start()

    def part_copy(k):
        return copies.make(slot_part[k], part_t.at[k], part_in.at[k], across)

    def backward(t):
        @pl.when(core != t)
        def _():
            for i in range(2):
                top_copy(t, i).wait_recv()

        top_pair = jnp.concatenate(split(jnp.concatenate([top_t[t, 0], top_t[t, 1]], axis=1)), axis=0)
        for k in (2, 3, 0, 1):
            cols = pl.ds(k * 256, 256)
            share = tall_product(top_pair, tiles_high[t, :, cols], tiles_low[t, :, cols])
            part_t[k] = share if t == 0 else part_t[k] + share
            if t == 1 and k >= 2:
                copies.send(slot_part[k], part_t.at[k], part_in.at[k], across)
            elif t == 1:

                @pl.when(row == 1)
                def _():
                    part_copy(k).start()

    def each(t, step, *rest):
        for p in pair(t):
            step(p, *rest)

    each(0, swap_beside)
    each(0, send_own)
    each(1, swap_beside)
    each(1, send_own)
    loads[1].wait()
    low_share()
    each(0, wait_beside)
    each(0, send_side)
    each(0, send_unit, 0)
    low_send()
    each(1, wait_beside)
    each(1, send_side)
    for s in (1, -1):
        each(0, relay_one, s)
    for s in (1, -1):
        each(0, send_unit, s)
    each(0, relay_two, 0)
    each(0, wait_far)
    each(0, send_unit, 2)
    each(1, send_unit, 0)
    invert_split(1)
    for s in (1, -1):
        each(0, relay_two, s)
    for s in (1, -1):
        each(1, relay_one, s)
    each(0, relay_two, 2)
    for s in (1, -1):
        each(1, send_unit, s)
    each(1, relay_two, 0)
    low_sum()
    each(1, wait_far)
    each(1, send_unit, 2)
    for u in units:
        each(0, wait_two_far, u)
    forward(0, (0, 1))
    each(1, relay_two, 1)
    forward(0, (2, 3))
    each(1, relay_two, -1)
    level_one_down(0)
    each(1, relay_two, 2)
    for u in units:
        each(1, wait_two_far, u)
    forward(1, range(4))
    level_one_down(1)
    level_one_up(0)
    top_out(0)
    backward(0)
    low_t[...] = low_in[...].T
    level_one_up(1)
    backward(1)
    top_out(1)

    def final(k):
        cols = pl.ds(k * 256, 256)
        copies.arrived(slot_part[k], part_in.at[k], across)
        target = low_t[:, cols] - part_t[k] - part_in[k]
        pair_ = jnp.concatenate(split(target), axis=0)
        return tall_product(pair_, inv_high[0, cols], inv_low[0, cols])

    answer_t[...] = final(2) + final(3)

    @pl.when(row == 0)
    def _():
        answer_t[...] = answer_t[...] + final(0)
        answer_t[...] = answer_t[...] + final(1)

    answers[0] = answer_t[...].T
    write_out(0).start()

    copies.finish()
    for t in range(2):

        @pl.when(core == t)
        def _():
            for i in range(4):
                update_copy(1 - t, i).wait_send()
            for i in range(2):
                top_copy(t, i).wait_send()

    @pl.when(row == 0)
    def _():
        copies.make(slot_low[0], low.at[upper], low_in.at[upper], across).wait_send()

    @pl.when(row == 1)
    def _():
        for k in (0, 1):
            part_copy(k).wait_send()

    for m in range(2):
        write_out(m).wait()


def per_device(sources, factor, block_mask, inverse_diagonal):
    return pl.pallas_call(
        kernel,
        out_shape=jax.ShapeDtypeStruct(sources.shape, F32),
        in_specs=[
            pl.BlockSpec(memory_space=pltpu.HBM),
            pl.BlockSpec(memory_space=pltpu.HBM),
            pl.BlockSpec(memory_space=pltpu.SMEM),
            pl.BlockSpec(memory_space=pltpu.HBM),
        ],
        out_specs=pl.BlockSpec(memory_space=pltpu.HBM),
        scratch_shapes=[
            pltpu.VMEM((2, HALF, SHOTS), F32),
            pltpu.VMEM((2, 16, FULL), F32),
            pltpu.VMEM((2, FULL, HALF), F32),
            pltpu.VMEM((2, 2, 16, 2, 16, HALF), F32),
            pltpu.VMEM((2, HALF, FULL), BF16),
            pltpu.VMEM((2, HALF, FULL), BF16),
            pltpu.VMEM((2, FULL, HALF), BF16),
            pltpu.VMEM((2, FULL, HALF), BF16),
            pltpu.VMEM((FULL, SHOTS), F32),
            pltpu.VMEM((FULL, SHOTS), F32),
            pltpu.VMEM((FULL, 2 * SHOTS), BF16),
            pltpu.VMEM((SHOTS, FULL), F32),
            pltpu.VMEM((2, HALF, SHOTS), F32),
            pltpu.VMEM((HALF, SHOTS), F32),
            pltpu.VMEM((FULL, SHOTS), F32),
            pltpu.VMEM((HALF, SHOTS), F32),
            pltpu.VMEM((2, 2, SHOTS, 256), F32),
            pltpu.VMEM((4, SHOTS, 256), F32),
            pltpu.VMEM((4, SHOTS, 256), F32),
            pltpu.VMEM((SHOTS, HALF), F32),
            pltpu.VMEM((2, HALF, SHOTS), F32),
            pltpu.SemaphoreType.DMA((6,)),
            pltpu.SemaphoreType.DMA((COPIES,)),
            pltpu.SemaphoreType.DMA((COPIES,)),
        ],
        compiler_params=pltpu.CompilerParams(
            collective_id=0, has_side_effects=True, vmem_limit_bytes=60 * 2**20
        ),
        cost_estimate=pl.CostEstimate(
            flops=3 * 8 * FULL * FULL * SHOTS, bytes_accessed=6 * 2**20, transcendentals=0
        ),
    )(sources, factor, block_mask, inverse_diagonal)


def solution(mesh):
    placed = (
        P("depth", None, "rows", "shots"),
        P("depth", None, ("rows", "shots"), None),
        P("depth", None, None, None),
        P("depth", None, None, "rows"),
    )
    return jax.shard_map(
        per_device,
        mesh=mesh,
        in_specs=placed,
        out_specs=P("depth", None, "rows", "shots"),
        check_vma=False,
    )
```

```python
import jax
import jax.numpy as jnp
from jax import lax
from jax.experimental import pallas as pl
from jax.experimental.pallas import tpu as pltpu
from jax.sharding import PartitionSpec as P

MESH = pl.DeviceIdType.MESH
F32 = jnp.float32
BF16 = jnp.bfloat16
BLOCK = 128
DIRECT = (0, 1)
HALF = 512
FULL = 1024
SHOTS = 128


def split(x):
    high = x.astype(BF16)
    return high, (x - high.astype(F32)).astype(BF16)


def dot(a, b):
    return jnp.dot(a, b, preferred_element_type=F32)


def wide_product(a_high, a_low, b_pair):
    both = dot(a_high, b_pair)
    return both[:, :SHOTS] + both[:, SHOTS:] + dot(a_low, b_pair[:, :SHOTS])


def tall_product(a_pair, b_high, b_low):
    both = dot(a_pair, b_high)
    return both[:SHOTS] + both[SHOTS:] + dot(a_pair[:SHOTS], b_low)


class Copies:
    def __init__(self, send_sems, recv_sems):
        self.send_sems, self.recv_sems, self.count, self.sent = send_sems, recv_sems, 0, []

    def slot(self):
        self.count += 1
        return self.count - 1

    def make(self, slot, src, dst, device):
        return pltpu.make_async_remote_copy(
            src_ref=src,
            dst_ref=dst,
            send_sem=self.send_sems.at[slot],
            recv_sem=self.recv_sems.at[slot],
            device_id=device,
            device_id_type=MESH,
        )

    def send(self, slot, src, dst, device):
        copy = self.make(slot, src, dst, device)
        copy.start()
        self.sent.append(copy)

    def arrived(self, slot, dst, device):
        self.make(slot, dst, dst, device).wait_recv()

    def finish(self):
        for copy in self.sent:
            copy.wait_send()


COPIES = 112


def kernel(
    src_hbm,
    fac_hbm,
    mask_ref,
    inv_hbm,
    out_ref,
    src,
    fac,
    inv,
    tiles,
    tiles_high,
    tiles_low,
    inv_high,
    inv_low,
    low,
    low_in,
    low_pair,
    low_t,
    update,
    update_in,
    high_out,
    high_in,
    top_t,
    part_t,
    part_in,
    answer_t,
    answers,
    load_sems,
    send_sems,
    recv_sems,
):
    core = lax.axis_index("depth")
    row = lax.axis_index("rows")
    shot = lax.axis_index("shots")
    zy, xl = shot // 2, shot % 2
    z, y = zy // 4, zy % 4

    def at(dz, dy):
        return ((z + dz) % 4) * 4 + (y + dy) % 4

    def place(axis, step):
        return at(step, 0) if axis == 0 else at(0, step)

    def neighbour(axis, step):
        return (core, row, place(axis, step) * 2 + xl)

    beside = (core, row, zy * 2 + 1 - xl)
    across = (core, 1 - row, shot)
    twin = (1 - core, row, shot)

    loads = [
        pltpu.make_async_copy(fac_hbm.at[0], fac, load_sems.at[0]),
        pltpu.make_async_copy(src_hbm.at[0], src, load_sems.at[1]),
        pltpu.make_async_copy(inv_hbm.at[0, 0], inv.at[0], load_sems.at[2]),
        pltpu.make_async_copy(inv_hbm.at[0, 1], inv.at[1], load_sems.at[3]),
    ]
    for load in loads:
        load.start()

    barrier = pltpu.get_barrier_semaphore()
    partners = [neighbour(a, s) for a in (0, 1) for s in (1, -1)] + [beside, across, twin, neighbour(0, 2), neighbour(1, 2)]
    for partner in partners:
        pl.semaphore_signal(barrier, inc=1, device_id=partner, device_id_type=MESH)

    def invert_split(m):
        loads[2 + m].wait()

        @pl.loop(0, 4)
        def _(i):
            rows = pl.ds(pl.multiple_of(i * 256, 256), 256)
            inv_high[m, rows], inv_low[m, rows] = split(inv[m, rows])

    def write_out(m):
        return pltpu.make_async_copy(answers.at[m], out_ref.at[0, m], load_sems.at[4 + m])

    loads[0].wait()
    row_block = row * 4 + zy // 4
    for t in range(2):
        for k in range(8):
            scale = mask_ref[0, t, row_block, k].astype(F32)
            piece = fac[t, :, k * BLOCK : (k + 1) * BLOCK] * scale
            tiles[t, k // 4, zy, xl, :, (k % 4) * BLOCK : (k % 4 + 1) * BLOCK] = piece

    invert_split(0)
    pl.semaphore_wait(barrier, len(partners))

    copies = Copies(send_sems, recv_sems)
    parts = [(t, h) for t in range(2) for h in range(2)]
    first = {h: 1 - h for h in range(2)}
    slot_x = {p: copies.slot() for p in parts}
    slot_own = {(p, s): copies.slot() for p in parts for s in (1, -1)}
    slot_side = {(p, s): copies.slot() for p in parts for s in (1, -1)}
    slot_far = {(p, s): copies.slot() for p in parts for s in (1, -1)}
    units = (0, -1, 1, 2)
    slot_two = {(p, u, s): copies.slot() for p in parts for u in units for s in (1, -1)}
    slot_two_far = {(p, u, s): copies.slot() for p in parts for u in units for s in (1, -1)}
    slot_low = [copies.slot() for _ in range(2)]
    slot_update = [copies.slot() for _ in range(4)]
    slot_high = [copies.slot() for _ in range(2)]
    slot_top = [copies.slot() for _ in range(2)]
    slot_part = [copies.slot() for _ in range(4)]
    assert copies.count <= COPIES

    def unit_place(h, u, s):
        return at(s, u) if first[h] == 1 else at(u, s)

    def swap_beside(p):
        t, h = p
        piece = tiles.at[t, h, zy, xl]
        copies.send(slot_x[p], piece, piece, beside)

    def send_own(p):
        t, h = p
        piece = tiles.at[t, h, zy, xl]
        for s in (1, -1):
            copies.send(slot_own[p, s], piece, piece, neighbour(first[h], s))
        if t in DIRECT:
            copies.send(slot_far[p, 1], piece, piece, neighbour(first[h], 2))

    def wait_beside(p):
        t, h = p
        copies.arrived(slot_x[p], tiles.at[t, h, zy, 1 - xl], beside)

    def send_side(p):
        t, h = p
        piece = tiles.at[t, h, zy, 1 - xl]
        for s in (1, -1):
            copies.send(slot_side[p, s], piece, piece, neighbour(first[h], s))
        if t in DIRECT:
            copies.send(slot_far[p, -1], piece, piece, neighbour(first[h], 2))

    def send_unit(p, u):
        t, h = p
        piece = tiles.at[t, h, unit_place(h, u, 0)]
        for s in (1, -1):
            copies.send(slot_two[p, u, s], piece, piece, neighbour(1 - first[h], s))
        if t == 1 and u == 2:
            copies.send(slot_two_far[p, u, 1], piece, piece, neighbour(1 - first[h], 2))

    def relay_one(p, s):
        t, h = p
        where = unit_place(h, -s, 0)
        copies.arrived(slot_own[p, s], tiles.at[t, h, where, xl], neighbour(first[h], -s))
        copies.arrived(slot_side[p, s], tiles.at[t, h, where, 1 - xl], neighbour(first[h], -s))
        if t not in DIRECT:
            piece = tiles.at[t, h, where, 0 if s == 1 else 1]
            copies.send(slot_far[p, s], piece, piece, neighbour(first[h], s))

    def wait_far(p):
        t, h = p
        for s in (1, -1):
            which = 0 if s == 1 else 1
            if t in DIRECT:
                which = xl if s == 1 else 1 - xl
            piece = tiles.at[t, h, unit_place(h, 2, 0), which]
            copies.arrived(slot_far[p, s], piece, neighbour(first[h], 2))

    def relay_two(p, u):
        t, h = p
        for s in (1, -1):
            where = unit_place(h, u, -s)
            copies.arrived(slot_two[p, u, s], tiles.at[t, h, where], neighbour(1 - first[h], -s))
            if t == 1 and u == 2:
                continue
            piece = tiles.at[t, h, where, 0 if s == 1 else 1]
            copies.send(slot_two_far[p, u, s], piece, piece, neighbour(1 - first[h], s))

    def wait_two_far(p, u):
        t, h = p
        if t == 1 and u == 2:
            copies.arrived(slot_two_far[p, u, 1], tiles.at[t, h, unit_place(h, u, 2)], neighbour(1 - first[h], 2))
            return
        for s in (1, -1):
            piece = tiles.at[t, h, unit_place(h, u, 2), 0 if s == 1 else 1]
            copies.arrived(slot_two_far[p, u, s], piece, neighbour(1 - first[h], -s))

    def pair(t):
        return [(t, 0), (t, 1)]

    bottom, upper = pl.ds(HALF, HALF), pl.ds(0, HALF)

    def low_share():
        source_pair = jnp.concatenate(split(src[0]), axis=1)

        @pl.loop(0, 4)
        def _(i):
            rows = pl.ds(pl.multiple_of(i * 256, 256), 256)
            low[rows] = wide_product(inv_high[0, rows], inv_low[0, rows], source_pair)

    def low_send():
        copies.send(slot_low[1], low.at[bottom], low_in.at[bottom], across)

        @pl.when(row == 0)
        def _():
            copies.make(slot_low[0], low.at[upper], low_in.at[upper], across).start()

    def low_sum():
        copies.arrived(slot_low[1], low_in.at[bottom], across)

        @pl.when(row == 1)
        def _():
            copies.arrived(slot_low[0], low_in.at[upper], across)

        @pl.when(row == 0)
        def _():
            low_in[upper] = low[upper]

        low_in[bottom] = low[bottom] + low_in[bottom]
        low_pair[...] = jnp.concatenate(split(low_in[...]), axis=1)

    def layer(i):
        return (z + i) % 4

    def layer_rows(i):
        return pl.ds(pl.multiple_of(layer(i) * 128, 128), 128)

    def update_copy(t, i):
        rows = layer_rows(i)
        return copies.make(slot_update[i], update.at[t, rows], update_in.at[rows], twin)

    def forward(t, chunks):
        for i in chunks:
            rows = layer_rows(i)
            total = jnp.zeros((128, SHOTS), F32)
            for h in range(2):
                block = tiles[t, h, pl.ds(layer(i) * 4, 4)].reshape(128, HALF)
                high, rest = split(block)
                cols = pl.ds(h * HALF, HALF)
                tiles_high[t, rows, cols] = high
                tiles_low[t, rows, cols] = rest
                total += wide_product(high, rest, low_pair[cols])
            update[t, rows] = total

            @pl.when(core != t)
            def _():
                update_copy(t, i).start()

    def high_copy(i):
        rows = pl.ds(HALF + i * 256, 256)
        return copies.make(slot_high[i], high_out.at[rows], high_in.at[pl.ds(i * 256, 256)], across)

    def level_one_down(t):
        @pl.when(core == t)
        def _():
            for i in range(4):
                update_copy(t, i).wait_recv()
            own_pair = jnp.concatenate(split(src[1] - update[t] - update_in[...]), axis=1)
            for i in (2, 3, 0, 1):
                rows = pl.ds(i * 256, 256)
                high_out[rows] = wide_product(inv_high[1, rows], inv_low[1, rows], own_pair)
                if i >= 2:
                    high_copy(i - 2).start()

    def top_copy(t, i):
        return copies.make(slot_top[i], top_t.at[t, i], top_t.at[t, i], twin)

    def level_one_up(t):
        @pl.when(core == t)
        def _():
            upper_pair = jnp.concatenate(split(high_out[upper].T), axis=0)
            halves = [pl.ds(i * 256, 256) for i in range(2)]
            for i in range(2):
                top_t[t, i] = tall_product(upper_pair, inv_high[1, upper, halves[i]], inv_low[1, upper, halves[i]])
            for i in range(2):
                high_copy(i).wait()
            lower_pair = jnp.concatenate(split((high_out[bottom] + high_in[...]).T), axis=0)
            for i in range(2):
                top_t[t, i] = top_t[t, i] + tall_product(
                    lower_pair, inv_high[1, bottom, halves[i]], inv_low[1, bottom, halves[i]]
                )
                top_copy(t, i).start()

    def top_out(t):
        @pl.when(core == t)
        def _():
            for i in range(2):
                answers[1, pl.ds(i * 256, 256)] = top_t[t, i].T
            write_out(1).start()

    def part_copy(k):
        return copies.make(slot_part[k], part_t.at[k], part_in.at[k], across)

    def backward(t):
        @pl.when(core != t)
        def _():
            for i in range(2):
                top_copy(t, i).wait_recv()

        top_pair = jnp.concatenate(split(jnp.concatenate([top_t[t, 0], top_t[t, 1]], axis=1)), axis=0)
        for k in (2, 3, 0, 1):
            cols = pl.ds(k * 256, 256)
            share = tall_product(top_pair, tiles_high[t, :, cols], tiles_low[t, :, cols])
            part_t[k] = share if t == 0 else part_t[k] + share
            if t == 1 and k >= 2:
                copies.send(slot_part[k], part_t.at[k], part_in.at[k], across)
            elif t == 1:

                @pl.when(row == 1)
                def _():
                    part_copy(k).start()

    def each(t, step, *rest):
        for p in pair(t):
            step(p, *rest)

    each(0, swap_beside)
    each(0, send_own)
    each(1, swap_beside)
    each(1, send_own)
    loads[1].wait()
    low_share()
    each(0, wait_beside)
    each(0, send_side)
    each(0, send_unit, 0)
    low_send()
    each(1, wait_beside)
    each(1, send_side)
    for s in (1, -1):
        each(0, relay_one, s)
    for s in (1, -1):
        each(0, send_unit, s)
    each(0, relay_two, 0)
    each(0, wait_far)
    each(0, send_unit, 2)
    each(1, send_unit, 0)
    invert_split(1)
    for s in (1, -1):
        each(0, relay_two, s)
    for s in (1, -1):
        each(1, relay_one, s)
    each(0, relay_two, 2)
    for s in (1, -1):
        each(1, send_unit, s)
    each(1, relay_two, 0)
    low_sum()
    each(1, wait_far)
    each(1, send_unit, 2)
    for u in units:
        each(0, wait_two_far, u)
    forward(0, (0, 1))
    each(1, relay_two, 1)
    forward(0, (2, 3))
    each(1, relay_two, -1)
    level_one_down(0)
    each(1, wait_two_far, 0)
    forward(1, (0,))
    each(1, relay_two, 2)
    each(1, wait_two_far, 1)
    each(1, wait_two_far, -1)
    forward(1, (1, 3))
    each(1, wait_two_far, 2)
    forward(1, (2,))
    level_one_down(1)
    level_one_up(0)
    top_out(0)
    backward(0)
    low_t[...] = low_in[...].T
    level_one_up(1)
    backward(1)
    top_out(1)

    def final(k):
        cols = pl.ds(k * 256, 256)
        copies.arrived(slot_part[k], part_in.at[k], across)
        target = low_t[:, cols] - part_t[k] - part_in[k]
        pair_ = jnp.concatenate(split(target), axis=0)
        return tall_product(pair_, inv_high[0, cols], inv_low[0, cols])

    answer_t[...] = final(2) + final(3)

    @pl.when(row == 0)
    def _():
        answer_t[...] = answer_t[...] + final(0)
        answer_t[...] = answer_t[...] + final(1)

    answers[0] = answer_t[...].T
    write_out(0).start()

    copies.finish()
    for t in range(2):

        @pl.when(core == t)
        def _():
            for i in range(4):
                update_copy(1 - t, i).wait_send()
            for i in range(2):
                top_copy(t, i).wait_send()

    @pl.when(row == 0)
    def _():
        copies.make(slot_low[0], low.at[upper], low_in.at[upper], across).wait_send()

    @pl.when(row == 1)
    def _():
        for k in (0, 1):
            part_copy(k).wait_send()

    for m in range(2):
        write_out(m).wait()


def per_device(sources, factor, block_mask, inverse_diagonal):
    return pl.pallas_call(
        kernel,
        out_shape=jax.ShapeDtypeStruct(sources.shape, F32),
        in_specs=[
            pl.BlockSpec(memory_space=pltpu.HBM),
            pl.BlockSpec(memory_space=pltpu.HBM),
            pl.BlockSpec(memory_space=pltpu.SMEM),
            pl.BlockSpec(memory_space=pltpu.HBM),
        ],
        out_specs=pl.BlockSpec(memory_space=pltpu.HBM),
        scratch_shapes=[
            pltpu.VMEM((2, HALF, SHOTS), F32),
            pltpu.VMEM((2, 16, FULL), F32),
            pltpu.VMEM((2, FULL, HALF), F32),
            pltpu.VMEM((2, 2, 16, 2, 16, HALF), F32),
            pltpu.VMEM((2, HALF, FULL), BF16),
            pltpu.VMEM((2, HALF, FULL), BF16),
            pltpu.VMEM((2, FULL, HALF), BF16),
            pltpu.VMEM((2, FULL, HALF), BF16),
            pltpu.VMEM((FULL, SHOTS), F32),
            pltpu.VMEM((FULL, SHOTS), F32),
            pltpu.VMEM((FULL, 2 * SHOTS), BF16),
            pltpu.VMEM((SHOTS, FULL), F32),
            pltpu.VMEM((2, HALF, SHOTS), F32),
            pltpu.VMEM((HALF, SHOTS), F32),
            pltpu.VMEM((FULL, SHOTS), F32),
            pltpu.VMEM((HALF, SHOTS), F32),
            pltpu.VMEM((2, 2, SHOTS, 256), F32),
            pltpu.VMEM((4, SHOTS, 256), F32),
            pltpu.VMEM((4, SHOTS, 256), F32),
            pltpu.VMEM((SHOTS, HALF), F32),
            pltpu.VMEM((2, HALF, SHOTS), F32),
            pltpu.SemaphoreType.DMA((6,)),
            pltpu.SemaphoreType.DMA((COPIES,)),
            pltpu.SemaphoreType.DMA((COPIES,)),
        ],
        compiler_params=pltpu.CompilerParams(
            collective_id=0, has_side_effects=True, vmem_limit_bytes=60 * 2**20
        ),
        cost_estimate=pl.CostEstimate(
            flops=3 * 8 * FULL * FULL * SHOTS, bytes_accessed=6 * 2**20, transcendentals=0
        ),
    )(sources, factor, block_mask, inverse_diagonal)


def solution(mesh):
    placed = (
        P("depth", None, "rows", "shots"),
        P("depth", None, ("rows", "shots"), None),
        P("depth", None, None, None),
        P("depth", None, None, "rows"),
    )
    return jax.shard_map(
        per_device,
        mesh=mesh,
        in_specs=placed,
        out_specs=P("depth", None, "rows", "shots"),
        check_vma=False,
    )
```

```python
import jax
import jax.numpy as jnp
from jax import lax
from jax.experimental import pallas as pl
from jax.experimental.pallas import tpu as pltpu
from jax.sharding import PartitionSpec as P

MESH = pl.DeviceIdType.MESH
F32 = jnp.float32
BF16 = jnp.bfloat16
BLOCK = 128
DIRECT = (0, 1)
HALF = 512
FULL = 1024
SHOTS = 128


def split(x):
    high = x.astype(BF16)
    return high, (x - high.astype(F32)).astype(BF16)


def dot(a, b):
    return jnp.dot(a, b, preferred_element_type=F32)


def wide_product(a_high, a_low, b_pair):
    both = dot(a_high, b_pair)
    return both[:, :SHOTS] + both[:, SHOTS:] + dot(a_low, b_pair[:, :SHOTS])


def tall_product(a_pair, b_high, b_low):
    both = dot(a_pair, b_high)
    return both[:SHOTS] + both[SHOTS:] + dot(a_pair[:SHOTS], b_low)


class Copies:
    def __init__(self, send_sems, recv_sems):
        self.send_sems, self.recv_sems, self.count, self.sent = send_sems, recv_sems, 0, []

    def slot(self):
        self.count += 1
        return self.count - 1

    def make(self, slot, src, dst, device):
        return pltpu.make_async_remote_copy(
            src_ref=src,
            dst_ref=dst,
            send_sem=self.send_sems.at[slot],
            recv_sem=self.recv_sems.at[slot],
            device_id=device,
            device_id_type=MESH,
        )

    def send(self, slot, src, dst, device):
        copy = self.make(slot, src, dst, device)
        copy.start()
        self.sent.append(copy)

    def arrived(self, slot, dst, device):
        self.make(slot, dst, dst, device).wait_recv()

    def finish(self):
        for copy in self.sent:
            copy.wait_send()


COPIES = 112


def kernel(
    src_hbm,
    fac_hbm,
    mask_ref,
    inv_hbm,
    out_ref,
    src,
    fac,
    inv,
    tiles,
    tiles_high,
    tiles_low,
    inv_high,
    inv_low,
    low,
    low_in,
    low_pair,
    low_t,
    update,
    update_in,
    high_out,
    high_in,
    top_t,
    part_t,
    part_in,
    answer_t,
    answers,
    load_sems,
    send_sems,
    recv_sems,
):
    core = lax.axis_index("depth")
    row = lax.axis_index("rows")
    shot = lax.axis_index("shots")
    zy, xl = shot // 2, shot % 2
    z, y = zy // 4, zy % 4

    def at(dz, dy):
        return ((z + dz) % 4) * 4 + (y + dy) % 4

    def place(axis, step):
        return at(step, 0) if axis == 0 else at(0, step)

    def neighbour(axis, step):
        return (core, row, place(axis, step) * 2 + xl)

    beside = (core, row, zy * 2 + 1 - xl)
    across = (core, 1 - row, shot)
    twin = (1 - core, row, shot)

    loads = [
        pltpu.make_async_copy(fac_hbm.at[0], fac, load_sems.at[0]),
        pltpu.make_async_copy(src_hbm.at[0], src, load_sems.at[1]),
        pltpu.make_async_copy(inv_hbm.at[0, 0], inv.at[0], load_sems.at[2]),
        pltpu.make_async_copy(inv_hbm.at[0, 1], inv.at[1], load_sems.at[3]),
    ]
    for load in loads:
        load.start()

    barrier = pltpu.get_barrier_semaphore()
    partners = [neighbour(a, s) for a in (0, 1) for s in (1, -1)] + [beside, across, twin, neighbour(0, 2), neighbour(1, 2)]
    for partner in partners:
        pl.semaphore_signal(barrier, inc=1, device_id=partner, device_id_type=MESH)

    def invert_split(m):
        loads[2 + m].wait()

        @pl.loop(0, 4)
        def _(i):
            rows = pl.ds(pl.multiple_of(i * 256, 256), 256)
            inv_high[m, rows], inv_low[m, rows] = split(inv[m, rows])

    def write_out(m):
        return pltpu.make_async_copy(answers.at[m], out_ref.at[0, m], load_sems.at[4 + m])

    loads[0].wait()
    row_block = row * 4 + zy // 4
    for t in range(2):
        for k in range(8):
            scale = mask_ref[0, t, row_block, k].astype(F32)
            piece = fac[t, :, k * BLOCK : (k + 1) * BLOCK] * scale
            tiles[t, k // 4, zy, xl, :, (k % 4) * BLOCK : (k % 4 + 1) * BLOCK] = piece

    invert_split(0)
    pl.semaphore_wait(barrier, len(partners))

    copies = Copies(send_sems, recv_sems)
    parts = [(t, h) for t in range(2) for h in range(2)]
    first = {h: 1 - h for h in range(2)}
    slot_x = {p: copies.slot() for p in parts}
    slot_own = {(p, s): copies.slot() for p in parts for s in (1, -1)}
    slot_side = {(p, s): copies.slot() for p in parts for s in (1, -1)}
    slot_far = {(p, s): copies.slot() for p in parts for s in (1, -1)}
    units = (0, -1, 1, 2)
    slot_two = {(p, u, s): copies.slot() for p in parts for u in units for s in (1, -1)}
    slot_two_far = {(p, u, s): copies.slot() for p in parts for u in units for s in (1, -1)}
    slot_low = [copies.slot() for _ in range(2)]
    slot_update = [copies.slot() for _ in range(4)]
    slot_high = [copies.slot() for _ in range(2)]
    slot_top = [copies.slot() for _ in range(2)]
    slot_part = [copies.slot() for _ in range(4)]
    assert copies.count <= COPIES

    def unit_place(h, u, s):
        return at(s, u) if first[h] == 1 else at(u, s)

    def swap_beside(p):
        t, h = p
        piece = tiles.at[t, h, zy, xl]
        copies.send(slot_x[p], piece, piece, beside)

    def send_own(p):
        t, h = p
        piece = tiles.at[t, h, zy, xl]
        for s in (1, -1):
            copies.send(slot_own[p, s], piece, piece, neighbour(first[h], s))
        if t in DIRECT:
            copies.send(slot_far[p, 1], piece, piece, neighbour(first[h], 2))

    def wait_beside(p):
        t, h = p
        copies.arrived(slot_x[p], tiles.at[t, h, zy, 1 - xl], beside)

    def send_side(p):
        t, h = p
        piece = tiles.at[t, h, zy, 1 - xl]
        for s in (1, -1):
            copies.send(slot_side[p, s], piece, piece, neighbour(first[h], s))
        if t in DIRECT:
            copies.send(slot_far[p, -1], piece, piece, neighbour(first[h], 2))

    def send_unit(p, u):
        t, h = p
        piece = tiles.at[t, h, unit_place(h, u, 0)]
        for s in (1, -1):
            copies.send(slot_two[p, u, s], piece, piece, neighbour(1 - first[h], s))
        if t == 1 and u == 2:
            copies.send(slot_two_far[p, u, 1], piece, piece, neighbour(1 - first[h], 2))

    def relay_one(p, s):
        t, h = p
        where = unit_place(h, -s, 0)
        copies.arrived(slot_own[p, s], tiles.at[t, h, where, xl], neighbour(first[h], -s))
        copies.arrived(slot_side[p, s], tiles.at[t, h, where, 1 - xl], neighbour(first[h], -s))
        if t not in DIRECT:
            piece = tiles.at[t, h, where, 0 if s == 1 else 1]
            copies.send(slot_far[p, s], piece, piece, neighbour(first[h], s))

    def wait_far(p):
        t, h = p
        for s in (1, -1):
            which = 0 if s == 1 else 1
            if t in DIRECT:
                which = xl if s == 1 else 1 - xl
            piece = tiles.at[t, h, unit_place(h, 2, 0), which]
            copies.arrived(slot_far[p, s], piece, neighbour(first[h], 2))

    def relay_two(p, u):
        t, h = p
        for s in (1, -1):
            where = unit_place(h, u, -s)
            copies.arrived(slot_two[p, u, s], tiles.at[t, h, where], neighbour(1 - first[h], -s))
            if t == 1 and u == 2:
                continue
            piece = tiles.at[t, h, where, 0 if s == 1 else 1]
            copies.send(slot_two_far[p, u, s], piece, piece, neighbour(1 - first[h], s))

    def wait_two_far(p, u):
        t, h = p
        if t == 1 and u == 2:
            copies.arrived(slot_two_far[p, u, 1], tiles.at[t, h, unit_place(h, u, 2)], neighbour(1 - first[h], 2))
            return
        for s in (1, -1):
            piece = tiles.at[t, h, unit_place(h, u, 2), 0 if s == 1 else 1]
            copies.arrived(slot_two_far[p, u, s], piece, neighbour(1 - first[h], -s))

    def pair(t):
        return [(t, 0), (t, 1)]

    bottom, upper = pl.ds(HALF, HALF), pl.ds(0, HALF)

    def low_share():
        source_pair = jnp.concatenate(split(src[0]), axis=1)

        @pl.loop(0, 4)
        def _(i):
            rows = pl.ds(pl.multiple_of(i * 256, 256), 256)
            low[rows] = wide_product(inv_high[0, rows], inv_low[0, rows], source_pair)

    def low_send():
        copies.send(slot_low[1], low.at[bottom], low_in.at[bottom], across)

        @pl.when(row == 0)
        def _():
            copies.make(slot_low[0], low.at[upper], low_in.at[upper], across).start()

    def low_sum():
        copies.arrived(slot_low[1], low_in.at[bottom], across)

        @pl.when(row == 1)
        def _():
            copies.arrived(slot_low[0], low_in.at[upper], across)

        @pl.when(row == 0)
        def _():
            low_in[upper] = low[upper]

        low_in[bottom] = low[bottom] + low_in[bottom]
        low_pair[...] = jnp.concatenate(split(low_in[...]), axis=1)

    def layer(i):
        return (z + i) % 4

    def layer_rows(i):
        return pl.ds(pl.multiple_of(layer(i) * 128, 128), 128)

    def update_copy(t, i):
        rows = layer_rows(i)
        return copies.make(slot_update[i], update.at[t, rows], update_in.at[rows], twin)

    def forward(t, chunks):
        for i in chunks:
            rows = layer_rows(i)
            total = jnp.zeros((128, SHOTS), F32)
            for h in range(2):
                block = tiles[t, h, pl.ds(layer(i) * 4, 4)].reshape(128, HALF)
                high, rest = split(block)
                cols = pl.ds(h * HALF, HALF)
                tiles_high[t, rows, cols] = high
                tiles_low[t, rows, cols] = rest
                total += wide_product(high, rest, low_pair[cols])
            update[t, rows] = total

            @pl.when(core != t)
            def _():
                update_copy(t, i).start()

    def high_copy(i):
        rows = pl.ds(HALF + i * 256, 256)
        return copies.make(slot_high[i], high_out.at[rows], high_in.at[pl.ds(i * 256, 256)], across)

    def level_one_down(t):
        @pl.when(core == t)
        def _():
            for i in range(4):
                update_copy(t, i).wait_recv()
            own_pair = jnp.concatenate(split(src[1] - update[t] - update_in[...]), axis=1)
            for i in (2, 3, 0, 1):
                rows = pl.ds(i * 256, 256)
                high_out[rows] = wide_product(inv_high[1, rows], inv_low[1, rows], own_pair)
                if i >= 2:
                    high_copy(i - 2).start()

    def top_copy(t, i):
        return copies.make(slot_top[i], top_t.at[t, i], top_t.at[t, i], twin)

    def level_one_up(t):
        @pl.when(core == t)
        def _():
            upper_pair = jnp.concatenate(split(high_out[upper].T), axis=0)
            halves = [pl.ds(i * 256, 256) for i in range(2)]
            for i in range(2):
                top_t[t, i] = tall_product(upper_pair, inv_high[1, upper, halves[i]], inv_low[1, upper, halves[i]])
            for c in range(2):
                high_copy(c).wait()
                rows = pl.ds(HALF + c * 256, 256)
                lower = (high_out[rows] + high_in[pl.ds(c * 256, 256)]).T
                lower_pair = jnp.concatenate(split(lower), axis=0)
                for i in range(2):
                    top_t[t, i] = top_t[t, i] + tall_product(
                        lower_pair, inv_high[1, rows, halves[i]], inv_low[1, rows, halves[i]]
                    )
                    if c == 1:
                        top_copy(t, i).start()

    def top_out(t):
        @pl.when(core == t)
        def _():
            for i in range(2):
                answers[1, pl.ds(i * 256, 256)] = top_t[t, i].T
            write_out(1).start()

    def part_copy(k):
        return copies.make(slot_part[k], part_t.at[k], part_in.at[k], across)

    def backward(t):
        @pl.when(core != t)
        def _():
            for i in range(2):
                top_copy(t, i).wait_recv()

        top_pair = jnp.concatenate(split(jnp.concatenate([top_t[t, 0], top_t[t, 1]], axis=1)), axis=0)
        for k in (2, 3, 0, 1):
            cols = pl.ds(k * 256, 256)
            share = tall_product(top_pair, tiles_high[t, :, cols], tiles_low[t, :, cols])
            part_t[k] = share if t == 0 else part_t[k] + share
            if t == 1 and k >= 2:
                copies.send(slot_part[k], part_t.at[k], part_in.at[k], across)
            elif t == 1:

                @pl.when(row == 1)
                def _():
                    part_copy(k).start()

    def each(t, step, *rest):
        for p in pair(t):
            step(p, *rest)

    each(0, swap_beside)
    each(0, send_own)
    each(1, swap_beside)
    each(1, send_own)
    loads[1].wait()
    low_share()
    each(0, wait_beside)
    each(0, send_side)
    each(0, send_unit, 0)
    low_send()
    each(1, wait_beside)
    each(1, send_side)
    for s in (1, -1):
        each(0, relay_one, s)
    for s in (1, -1):
        each(0, send_unit, s)
    each(0, relay_two, 0)
    each(0, wait_far)
    each(0, send_unit, 2)
    each(1, send_unit, 0)
    invert_split(1)
    for s in (1, -1):
        each(0, relay_two, s)
    for s in (1, -1):
        each(1, relay_one, s)
    each(0, relay_two, 2)
    for s in (1, -1):
        each(1, send_unit, s)
    each(1, relay_two, 0)
    low_sum()
    each(1, wait_far)
    each(1, send_unit, 2)
    for u in units:
        each(0, wait_two_far, u)
    forward(0, (0, 1))
    each(1, relay_two, 1)
    forward(0, (2, 3))
    each(1, relay_two, -1)
    level_one_down(0)
    each(1, wait_two_far, 0)
    forward(1, (0,))
    each(1, relay_two, 2)
    each(1, wait_two_far, 1)
    each(1, wait_two_far, -1)
    forward(1, (1, 3))
    each(1, wait_two_far, 2)
    forward(1, (2,))
    level_one_down(1)
    level_one_up(0)
    top_out(0)
    backward(0)
    low_t[...] = low_in[...].T
    level_one_up(1)
    backward(1)
    top_out(1)

    def final(k):
        cols = pl.ds(k * 256, 256)
        copies.arrived(slot_part[k], part_in.at[k], across)
        target = low_t[:, cols] - part_t[k] - part_in[k]
        pair_ = jnp.concatenate(split(target), axis=0)
        return tall_product(pair_, inv_high[0, cols], inv_low[0, cols])

    answer_t[...] = final(2) + final(3)

    @pl.when(row == 0)
    def _():
        answer_t[...] = answer_t[...] + final(0)
        answer_t[...] = answer_t[...] + final(1)

    answers[0] = answer_t[...].T
    write_out(0).start()

    copies.finish()
    for t in range(2):

        @pl.when(core == t)
        def _():
            for i in range(4):
                update_copy(1 - t, i).wait_send()
            for i in range(2):
                top_copy(t, i).wait_send()

    @pl.when(row == 0)
    def _():
        copies.make(slot_low[0], low.at[upper], low_in.at[upper], across).wait_send()

    @pl.when(row == 1)
    def _():
        for k in (0, 1):
            part_copy(k).wait_send()

    for m in range(2):
        write_out(m).wait()


def per_device(sources, factor, block_mask, inverse_diagonal):
    return pl.pallas_call(
        kernel,
        out_shape=jax.ShapeDtypeStruct(sources.shape, F32),
        in_specs=[
            pl.BlockSpec(memory_space=pltpu.HBM),
            pl.BlockSpec(memory_space=pltpu.HBM),
            pl.BlockSpec(memory_space=pltpu.SMEM),
            pl.BlockSpec(memory_space=pltpu.HBM),
        ],
        out_specs=pl.BlockSpec(memory_space=pltpu.HBM),
        scratch_shapes=[
            pltpu.VMEM((2, HALF, SHOTS), F32),
            pltpu.VMEM((2, 16, FULL), F32),
            pltpu.VMEM((2, FULL, HALF), F32),
            pltpu.VMEM((2, 2, 16, 2, 16, HALF), F32),
            pltpu.VMEM((2, HALF, FULL), BF16),
            pltpu.VMEM((2, HALF, FULL), BF16),
            pltpu.VMEM((2, FULL, HALF), BF16),
            pltpu.VMEM((2, FULL, HALF), BF16),
            pltpu.VMEM((FULL, SHOTS), F32),
            pltpu.VMEM((FULL, SHOTS), F32),
            pltpu.VMEM((FULL, 2 * SHOTS), BF16),
            pltpu.VMEM((SHOTS, FULL), F32),
            pltpu.VMEM((2, HALF, SHOTS), F32),
            pltpu.VMEM((HALF, SHOTS), F32),
            pltpu.VMEM((FULL, SHOTS), F32),
            pltpu.VMEM((HALF, SHOTS), F32),
            pltpu.VMEM((2, 2, SHOTS, 256), F32),
            pltpu.VMEM((4, SHOTS, 256), F32),
            pltpu.VMEM((4, SHOTS, 256), F32),
            pltpu.VMEM((SHOTS, HALF), F32),
            pltpu.VMEM((2, HALF, SHOTS), F32),
            pltpu.SemaphoreType.DMA((6,)),
            pltpu.SemaphoreType.DMA((COPIES,)),
            pltpu.SemaphoreType.DMA((COPIES,)),
        ],
        compiler_params=pltpu.CompilerParams(
            collective_id=0, has_side_effects=True, vmem_limit_bytes=60 * 2**20
        ),
        cost_estimate=pl.CostEstimate(
            flops=3 * 8 * FULL * FULL * SHOTS, bytes_accessed=6 * 2**20, transcendentals=0
        ),
    )(sources, factor, block_mask, inverse_diagonal)


def solution(mesh):
    placed = (
        P("depth", None, "rows", "shots"),
        P("depth", None, ("rows", "shots"), None),
        P("depth", None, None, None),
        P("depth", None, None, "rows"),
    )
    return jax.shard_map(
        per_device,
        mesh=mesh,
        in_specs=placed,
        out_specs=P("depth", None, "rows", "shots"),
        check_vma=False,
    )
```
